32 devices in a mesh: groups: 2 (over y), lon: 4 (over z), chan: 2 (over x), lat: 2 (over core).
Axes of the slice: x: 2, y: 2, z: 4, core: 2. Of those that a mesh axis runs over, the one named last changes fastest.
Arguments:
- inputs: bfloat16 [256, 64, 512], P('chan', ('groups', 'lat'), 'lon'), parts along dimension 1, may hold values from -6 to 6
- cotangent: bfloat16 [256, 64, 512], P('chan', ('groups', 'lat'), 'lon'), parts along dimension 1, may hold values from -6 to 6
- weight: bfloat16 [3, 3, 256, 256], P(None, None, 'chan'), may hold values from -0.125 to 0.125
- bias_vector: float32 [256], P('chan'), may hold values from -4 to 4
Outputs:
- input_grad: bfloat16 [256, 64, 512], P('chan', ('groups', 'lat'), 'lon'), parts along dimension 1
- weight_grad: float32 [6, 3, 256, 256], P('groups', None, 'chan'), parts along dimension 0
- bias_grad: float32 [512], P(('groups', 'chan')), parts along dimension 0
The draws below stay inside these ranges and needn't reach their ends.
There are 2 independent parts, one for each index of `groups`. The reference program is written for one: setup_inputs(seed, part) draws one part's arguments, and reference() takes and returns one part's arrays. A program takes and returns all parts, laid end to end along the dimension named above; an argument that names none is the same for every part. Nothing has to cross between parts.
All inputs are finite; a program needn't handle non-finite values.
Results may differ from the reference program's by a relative error of at most 0.007.
Values may be sent and summed in bfloat16 or wider, within the bound.
A program may use at most 64 MiB of HBM per device.

```python
import jax
import jax.numpy as jnp
from jax import lax

C = 256
HEIGHT = 32
WIDTH = 512


def level_of(rng, shape, shards, low, high):
    def one(axis_at, blocks):
        draws = jax.random.uniform(jax.random.fold_in(jax.random.fold_in(rng, 6), axis_at), (blocks,), jnp.float32, low / len(shards), high / len(shards))
        return jnp.repeat(jnp.exp(draws), shape[axis_at] // blocks).reshape((-1,) + (1,) * (len(shape) - axis_at - 1))

    gain = one(*shards[0])
    for cut in shards[1:]:
        gain = gain * one(*cut)
    return gain


def bell_draw(key, extent, scale, bound, cuts=(), held_as=jnp.bfloat16):
    result = jax.random.normal(key, extent, jnp.float32) * scale
    if len(cuts) > 0:
        result = level_of(key, extent, cuts, -0.22, 0.18) * result
    return jnp.clip(result, min=-bound, max=bound).astype(held_as)


def setup_inputs(seed: int = 0, part: int = 0) -> dict:
    key_of = jax.random.split(jax.random.key(seed), 5)
    own_keys = jax.random.split(jax.random.fold_in(key_of[4], part), 5)
    return {
        "inputs": bell_draw(own_keys[0], (C, HEIGHT, WIDTH), 1.0, 6.0, ((0, 2), (1, 2), (2, 4))),
        "cotangent": bell_draw(own_keys[1], (C, HEIGHT, WIDTH), 1.0, 6.0, ((0, 2), (1, 2), (2, 4))),
        "weight": bell_draw(key_of[2], (3, 3, C, C), (9 * C) ** -0.5, 0.125, ((2, 2),)),
        "bias_vector": bell_draw(key_of[3], (C,), 1.0, 4.0, ((0, 2),), jnp.float32),
    }


def pad_field(field):
    wrapped = jnp.concatenate([field[:, :, -1:], field, field[:, :, :1]], axis=2)
    return jnp.pad(wrapped, ((0, 0), (1, 1), (0, 0)))


def gelu_slope(preact):
    normal_cdf = 0.5 * (1.0 + jax.scipy.special.erf(preact * 0.7071067811865476))
    density = jnp.exp(-0.5 * preact * preact) * 0.3989422804014327
    return normal_cdf + preact * density


def reference(inputs, cotangent, weight, bias_vector):
    channels, height, breadth = inputs.shape
    padded = pad_field(inputs).astype(jnp.float32)
    kernel = weight.astype(jnp.float32)
    preact = jnp.zeros((channels, height * breadth), jnp.float32)
    for tap_row in range(3):
        for tap_col in range(3):
            window = padded[:, tap_row:tap_row + height, tap_col:tap_col + breadth].reshape(channels, -1)
            preact = preact + jnp.dot(kernel[tap_row, tap_col], window, precision=lax.Precision.HIGHEST)
    preact = preact + bias_vector[:, None]
    upstream = cotangent.reshape(channels, -1).astype(jnp.float32)
    grad_pre = (upstream * gelu_slope(preact)).astype(jnp.bfloat16)
    grad_wide = grad_pre.astype(jnp.float32)
    bias_grad = jnp.sum(grad_wide, axis=1)
    taps = []
    for tap_row in range(3):
        row_taps = []
        for tap_col in range(3):
            window = padded[:, tap_row:tap_row + height, tap_col:tap_col + breadth].reshape(channels, -1)
            row_taps.append(lax.dot_general(grad_wide, window, (((1,), (1,)), ((), ())), precision=lax.Precision.HIGHEST))
        taps.append(jnp.stack(row_taps))
    weight_grad = jnp.stack(taps)
    grad_padded = pad_field(grad_pre.reshape(channels, height, breadth)).astype(jnp.float32)
    summed = jnp.zeros((channels, height * breadth), jnp.float32)
    for tap_row in range(3):
        for tap_col in range(3):
            window = grad_padded[:, 2 - tap_row:2 - tap_row + height, 2 - tap_col:2 - tap_col + breadth].reshape(channels, -1)
            summed = summed + lax.dot_general(kernel[tap_row, tap_col], window, (((0,), (0,)), ((), ())), precision=lax.Precision.HIGHEST)
    input_grad = summed.astype(jnp.bfloat16).reshape(channels, height, breadth)
    return input_grad, weight_grad, bias_grad
```

```python
import functools

import jax
import jax.numpy as jnp
from jax import lax
from jax.experimental import pallas as pl
from jax.experimental.pallas import tpu as pltpu
from jax.sharding import PartitionSpec as P

MESH = pl.DeviceIdType.MESH
BF = jnp.bfloat16
F32 = jnp.float32
PIECES = 4


def gelu_slope(preact):
    normal_cdf = 0.5 * (1.0 + lax.erf(preact * 0.7071067811865476))
    density = jnp.exp(-0.5 * preact * preact) * 0.3989422804014327
    return normal_cdf + preact * density


def nt(a, b):
    return lax.dot_general(a, b, (((1,), (1,)), ((), ())), preferred_element_type=F32)


def kernel(
    sizes,
    x_ref, ct_ref, w_ref, b_ref,
    dx_ref, dw_ref, db_ref,
    xs, hx, hc, edge, shift, w2, wt, gs, hg, hgc, gedge,
    dwp, dwsend, dwcore, zsend, zrecv, gathered, bias, dxf, dxs, dxr,
    x_sem, row_sem, col_sem, grow_sem, gcol_sem, core_sem, rs_sem, ag_sem, fwd_sem, bias_sem, dx_sem,
):
    nlon, nchan, nlat, C, CA, H, W, R = sizes
    L = H * W
    part = L // PIECES
    group = lax.axis_index("groups")
    lon = lax.axis_index("lon")
    chan = lax.axis_index("chan")
    lat = lax.axis_index("lat")
    other = 1 - lat

    def at(a, b, c):
        return (group, a, b, c)

    def copy(src, dst, sems, index, device):
        return pltpu.make_async_remote_copy(
            src_ref=src, dst_ref=dst,
            send_sem=sems.at[(0,) + index], recv_sem=sems.at[(1,) + index],
            device_id=device, device_id_type=MESH,
        )

    everyone = nlon * nchan * nlat
    me = (lon * nchan + chan) * nlat + lat
    barrier = pltpu.get_barrier_semaphore()

    @pl.loop(1, everyone)
    def _(d):
        peer = lax.rem(me + d, everyone)
        pl.semaphore_signal(
            barrier, inc=1, device_id_type=MESH,
            device_id=at(peer // (nchan * nlat), lax.rem(peer // nlat, nchan), lax.rem(peer, nlat)),
        )

    def edges(field):
        row = lax.broadcasted_iota(jnp.int32, (2 * H, L), 0)
        lane = lax.broadcasted_iota(jnp.int32, (2 * H, L), 1)
        want = jnp.where(row < H, row * W, (row - H) * W + W - 1)
        pick = jnp.where(lane == want, 1.0, 0.0).astype(BF)
        return nt(pick, field).astype(BF)

    edge[...] = edges(x_ref[...])
    mine = pl.ds(pl.multiple_of(chan * C, C), C)
    xs[1, mine, pl.ds(W, L)] = x_ref[...]
    rim = pl.ds(pl.multiple_of(lat * (H + 1) * W, W), W)
    xs[1, :, rim] = jnp.zeros((CA, W), BF)
    gs[1, :, rim] = jnp.zeros((C, W), BF)
    pl.semaphore_wait(barrier, everyone - 1)

    from_row = pl.ds(pl.multiple_of(other * (H - 1) * W, W), W)
    to_row = pl.ds(pl.multiple_of(lat * 0 + (1 - other) * 0 + other * 0 + lat * (H + 1) * W, W), W)
    x_copies, halo_copies = [], []
    for d in range(nchan):
        there = lax.rem(chan + d, nchan)
        halo_copies.append(
            copy(x_ref.at[:, from_row], xs.at[1, mine, to_row], row_sem, (d,), at(lon, there, other))
        )
        for side in range(2):
            lon_to = lax.rem(lon + (nlon - 1 if side == 0 else 1), nlon)
            for dl in range(2):
                halo_copies.append(
                    copy(
                        edge.at[pl.ds(side * H, H)],
                        hx.at[chan, pl.ds(((1 - side) * 2 + dl) * H, H)],
                        col_sem, (d, side, dl),
                        at(lon_to, there, lat if dl == 0 else other),
                    )
                )
    for c in halo_copies:
        c.start()
    for piece in range(PIECES):
        for d in range(1, nchan):
            c = copy(
                x_ref.at[:, pl.ds(piece * part, part)],
                xs.at[1, mine, pl.ds(W + piece * part, part)],
                x_sem, (d, piece), at(lon, lax.rem(chan + d, nchan), lat),
            )
            c.start()
            x_copies.append(c)

    @pl.loop(0, H + 2)
    def _(r):
        k = lax.broadcasted_iota(jnp.int32, (W + 128, 2 * W), 0)
        n = lax.broadcasted_iota(jnp.int32, (W + 128, 2 * W), 1)
        first = jnp.where(lat == 1, 2 * H - 1, -1000)
        last = jnp.where(lat == 0, H, -1000)
        held = jnp.where(r == 0, first, jnp.where(r == H + 1, last, r - 1))
        right = n >= W
        col = jnp.where(right, n - W, n)
        want = jnp.where(right, col + 1, col - 1)
        want = jnp.where(right & (col == W - 1), W + 2 * H + held, want)
        want = jnp.where((~right) & (col == 0), W + held, want)
        hit = jnp.where(k == want, 1.0, 0.0).astype(BF)
        shift[:, pl.ds(pl.multiple_of(r * 2 * W, 2 * W), 2 * W)] = hit

    for t in range(9):
        w2[:, pl.ds(t * CA, CA)] = w_ref[pl.ds(t * C, C), :]
    wt[...] = jnp.transpose(w_ref[...].astype(F32)).astype(BF)

    def build_shifts(field, columns):
        @pl.loop(0, H + 2)
        def _(r):
            here = pl.ds(pl.multiple_of(r * W, W), W)
            both = jnp.concatenate([field[1, :, here], columns[...]], axis=1)
            moved = jnp.dot(
                both, shift[:, pl.ds(pl.multiple_of(r * 2 * W, 2 * W), 2 * W)],
                preferred_element_type=F32,
            ).astype(BF)
            field[0, :, here] = moved[:, :W]
            field[2, :, here] = moved[:, W:]

    def turned(block):
        full = jnp.concatenate([block, jnp.zeros((128 - block.shape[0], block.shape[1]), BF)], axis=0)
        return jnp.transpose(full.astype(F32)).astype(BF)

    for c in halo_copies:
        c.wait()
    for k in range(nchan):
        hc[pl.ds(k * C, C), :] = turned(hx[k])
    for c in x_copies:
        c.wait()
    build_shifts(xs, hc)

    @pl.loop(0, PIECES)
    def _(piece):
        def lanes(p):
            return pl.ds(pl.multiple_of(p * W + piece * part, W), part)

        stack = jnp.concatenate(
            [xs[q, :, lanes(p)] for p in range(3) for q in range(3)], axis=0
        )
        preact = jnp.dot(w2[...], stack, preferred_element_type=F32) + b_ref[...]
        upstream = ct_ref[:, lanes(0)].astype(F32)
        gs[1, :, lanes(1)] = (upstream * gelu_slope(preact)).astype(BF)

    gedge[...] = edges(gs[1, :, pl.ds(W, L)])
    grad_from = pl.ds(pl.multiple_of(W + other * (H - 1) * W, W), W)
    grad_copies = [copy(gs.at[1, :, grad_from], gs.at[1, :, to_row], grow_sem, (0,), at(lon, chan, other))]
    for side in range(2):
        lon_to = lax.rem(lon + (nlon - 1 if side == 0 else 1), nlon)
        for dl in range(2):
            grad_copies.append(
                copy(
                    gedge.at[pl.ds(side * H, H)],
                    hg.at[pl.ds(((1 - side) * 2 + dl) * H, H)],
                    gcol_sem, (side, dl), at(lon_to, chan, lat if dl == 0 else other),
                )
            )
    for c in grad_copies:
        c.start()

    ring = nlon * nlat
    spot = lon * nlat + lat
    bias[spot] = nt(jnp.ones((8, L), BF), gs[1, :, pl.ds(W, L)])
    bias_copies = []
    for d in range(1, ring):
        peer = lax.rem(spot + d, ring)
        c = copy(bias.at[spot], bias.at[spot], bias_sem, (d,), at(peer // nlat, chan, lax.rem(peer, nlat)))
        c.start()
        bias_copies.append(c)

    if R > 9 * C:
        dwp[pl.ds(9 * C, R - 9 * C), :] = jnp.zeros((R - 9 * C, CA), F32)
    for p in range(3):
        for q in range(3):
            dwp[pl.ds((p * 3 + q) * C, C), :] = nt(
                gs[1, :, pl.ds(W, L)], xs[q, :, pl.ds(p * W, L)]
            )
    half = R // 2
    quarter = half // nlon
    dwsend[...] = dwp[pl.ds(pl.multiple_of(other * half, half), half), :].astype(BF)
    core_copy = copy(dwsend, dwcore, core_sem, (0,), at(lon, chan, other))
    core_copy.start()

    for c in grad_copies:
        c.wait()
    hgc[...] = turned(hg[...])
    build_shifts(gs, hgc)

    @pl.loop(0, PIECES)
    def _(piece):
        def lanes(p):
            return pl.ds(pl.multiple_of(p * W + piece * part, W), part)

        stack = jnp.concatenate(
            [gs[2 - q, :, lanes(2 - p)] for p in range(3) for q in range(3)], axis=0
        )
        whole = jnp.dot(wt[...], stack, preferred_element_type=F32)
        dxf[:, lanes(0)] = whole
        dxs[:, lanes(0)] = whole.astype(BF)
        for d in range(1, nchan):
            there = lax.rem(chan + d, nchan)
            theirs = pl.ds(pl.multiple_of(there * C, C), C)
            copy(
                dxs.at[theirs, lanes(0)], dxr.at[d, :, lanes(0)], dx_sem, (d, piece), at(lon, there, lat)
            ).start()

    core_copy.wait()
    base = lat * half
    own_half = pl.ds(pl.multiple_of(base, half), half)
    summed = dwp[own_half, :] + dwcore[...].astype(F32)
    dwp[own_half, :] = summed
    zsend[...] = summed.astype(BF)
    rs_copies = []
    for d in range(1, nlon):
        there = lax.rem(lon + d, nlon)
        c = copy(
            zsend.at[pl.ds(pl.multiple_of(there * quarter, 16), quarter), :],
            zrecv.at[d], rs_sem, (d,), at(there, chan, lat),
        )
        c.start()
        rs_copies.append(c)
    for c in rs_copies:
        c.wait()
    own_rows = pl.ds(pl.multiple_of(base + lon * quarter, 16), quarter)
    total = dwp[own_rows, :]
    for d in range(1, nlon):
        total = total + zrecv[d].astype(F32)
    gathered[own_rows, :] = total.astype(BF)
    ag_copies, fwd_copies = [], []
    for d in range(1, nlon):
        c = copy(
            gathered.at[own_rows, :], gathered.at[own_rows, :], ag_sem, (d,),
            at(lax.rem(lon + d, nlon), chan, lat),
        )
        c.start()
        ag_copies.append(c)
    for d in range(nlon):
        if d > 0:
            ag_copies[d - 1].wait_recv()
        source = lax.rem(lon + nlon - d, nlon)
        rows = pl.ds(pl.multiple_of(base + source * quarter, 16), quarter)
        c = copy(gathered.at[rows, :], gathered.at[rows, :], fwd_sem, (d,), at(lon, chan, other))
        c.start()
        fwd_copies.append(c)

    for piece in range(PIECES):
        here = pl.ds(piece * part, part)
        acc = dxf[mine, here]
        for d in range(1, nchan):
            there = lax.rem(chan + d, nchan)
            theirs = pl.ds(pl.multiple_of(there * C, C), C)
            copy(dxs.at[theirs, here], dxr.at[d, :, here], dx_sem, (d, piece), at(lon, there, lat)).wait()
            acc = acc + dxr[d, :, here].astype(F32)
        dx_ref[:, here] = acc.astype(BF)

    for c in bias_copies:
        c.wait()
    db_ref[...] = jnp.sum(bias[...], axis=0)
    for c in ag_copies:
        c.wait_send()
    for c in fwd_copies:
        c.wait()
    dw_ref[...] = gathered[...]


def local(nlon, nchan, nlat, inputs, cotangent, weight, bias_vector):
    C, H, W = inputs.shape
    CA = weight.shape[3]
    L = H * W
    step = nlat * nlon * 16
    R = -(-9 * C // step) * step
    half = R // nlat
    sizes = (nlon, nchan, nlat, C, CA, H, W, R)
    wide = (H + 2) * W
    vmem = pl.BlockSpec(memory_space=pltpu.VMEM)
    dma = pltpu.SemaphoreType.DMA
    dx, dw, db = pl.pallas_call(
        functools.partial(kernel, sizes),
        out_shape=(
            jax.ShapeDtypeStruct((C, L), BF),
            jax.ShapeDtypeStruct((R, CA), BF),
            jax.ShapeDtypeStruct((8, C), F32),
        ),
        in_specs=[vmem] * 4,
        out_specs=(vmem,) * 3,
        scratch_shapes=[
            pltpu.VMEM((3, CA, wide), BF),
            pltpu.VMEM((nchan, 4 * H, C), BF),
            pltpu.VMEM((CA, 128), BF),
            pltpu.VMEM((2 * H, C), BF),
            pltpu.VMEM((W + 128, (H + 2) * 2 * W), BF),
            pltpu.VMEM((C, 9 * CA), BF),
            pltpu.VMEM((CA, 9 * C), BF),
            pltpu.VMEM((3, C, wide), BF),
            pltpu.VMEM((4 * H, C), BF),
            pltpu.VMEM((C, 128), BF),
            pltpu.VMEM((2 * H, C), BF),
            pltpu.VMEM((R, CA), F32),
            pltpu.VMEM((half, CA), BF),
            pltpu.VMEM((half, CA), BF),
            pltpu.VMEM((half, CA), BF),
            pltpu.VMEM((nlon, half // nlon, CA), BF),
            pltpu.VMEM((R, CA), BF),
            pltpu.VMEM((nlon * nlat, 8, C), F32),
            pltpu.VMEM((CA, L), F32),
            pltpu.VMEM((CA, L), BF),
            pltpu.VMEM((nchan, C, L), BF),
            dma((2, nchan, PIECES)),
            dma((2, nchan)),
            dma((2, nchan, 2, 2)),
            dma((2, 1)),
            dma((2, 2, 2)),
            dma((2, 1)),
            dma((2, nlon)),
            dma((2, nlon)),
            dma((2, nlon)),
            dma((2, nlon * nlat)),
            dma((2, nchan, PIECES)),
        ],
        compiler_params=pltpu.CompilerParams(
            collective_id=0, has_side_effects=True, vmem_limit_bytes=48 * 1024 * 1024
        ),
        cost_estimate=pl.CostEstimate(
            flops=3 * 2 * 9 * C * CA * L, bytes_accessed=4 * C * L * 2, transcendentals=2 * C * L
        ),
        name="conv_backward",
    )(
        inputs.reshape(C, L),
        cotangent.reshape(C, L),
        weight.reshape(9 * C, CA),
        bias_vector.reshape(C, 1),
    )
    weight_grad = dw[: 9 * C].astype(F32).reshape(3, 3, C, CA)
    return dx.reshape(C, H, W), weight_grad, db[0]


def solution(mesh):
    shape = mesh.shape
    placed = (
        P("chan", ("groups", "lat"), "lon"),
        P("chan", ("groups", "lat"), "lon"),
        P(None, None, "chan", None),
        P("chan"),
    )
    return jax.shard_map(
        functools.partial(local, shape["lon"], shape["chan"], shape["lat"]),
        mesh=mesh,
        in_specs=placed,
        out_specs=(
            P("chan", ("groups", "lat"), "lon"),
            P("groups", None, "chan", None),
            P(("groups", "chan")),
        ),
        check_vma=False,
    )
```

```python
import functools

import jax
import jax.numpy as jnp
from jax import lax
from jax.experimental import pallas as pl
from jax.experimental.pallas import tpu as pltpu
from jax.sharding import PartitionSpec as P

MESH = pl.DeviceIdType.MESH
BF = jnp.bfloat16
F32 = jnp.float32
PIECES = 4


def gelu_slope(preact):
    normal_cdf = 0.5 * (1.0 + lax.erf(preact * 0.7071067811865476))
    density = jnp.exp(-0.5 * preact * preact) * 0.3989422804014327
    return normal_cdf + preact * density


def nt(a, b):
    return lax.dot_general(a, b, (((1,), (1,)), ((), ())), preferred_element_type=F32)


def kernel(
    sizes,
    x_ref, ct_ref, w_ref, b_ref,
    dx_ref, dw_ref, db_ref,
    xs, hx, hc, edge, shift, w2, wt, gs, hg, hgo, gedge,
    dwp, dwsend, dwcore, zsend, zrecv, gathered, bias, dxf, dxs, dxr,
    x_sem, row_sem, col_sem, grow_sem, gcol_sem, gother_sem, core_sem, rs_sem, ag_sem, fwd_sem, bias_sem, dx_sem,
):
    nlon, nchan, nlat, C, CA, H, W, R = sizes
    L = H * W
    group = lax.axis_index("groups")
    lon = lax.axis_index("lon")
    chan = lax.axis_index("chan")
    lat = lax.axis_index("lat")
    other = 1 - lat

    def at(a, b, c):
        return (group, a, b, c)

    def copy(src, dst, sems, index, device):
        return pltpu.make_async_remote_copy(
            src_ref=src, dst_ref=dst,
            send_sem=sems.at[(0,) + index], recv_sem=sems.at[(1,) + index],
            device_id=device, device_id_type=MESH,
        )

    everyone = nlon * nchan * nlat
    me = (lon * nchan + chan) * nlat + lat
    barrier = pltpu.get_barrier_semaphore()

    @pl.loop(1, everyone)
    def _(d):
        peer = lax.rem(me + d, everyone)
        pl.semaphore_signal(
            barrier, inc=1, device_id_type=MESH,
            device_id=at(peer // (nchan * nlat), lax.rem(peer // nlat, nchan), lax.rem(peer, nlat)),
        )

    def edges(field, start):
        rows, lanes = 2 * H, field.shape[1]
        row = lax.broadcasted_iota(jnp.int32, (rows, lanes), 0)
        lane = lax.broadcasted_iota(jnp.int32, (rows, lanes), 1) + start * W
        want = jnp.where(row < H, row * W, (row - H) * W + W - 1)
        pick = jnp.where(lane == want, 1.0, 0.0).astype(BF)
        return nt(pick, field).astype(BF)

    def walk(start, count):
        return jnp.where(lat == 1, start, H - start - count)

    def cols(row, count):
        return pl.ds(pl.multiple_of(row * W, W), count * W)

    edge[...] = edges(x_ref[...], 0)
    mine = pl.ds(pl.multiple_of(chan * C, C), C)
    xs[1, mine, pl.ds(W, L)] = x_ref[...]
    rim = cols(lat * (H + 1), 1)
    for q in range(3):
        xs[q, :, rim] = jnp.zeros((CA, W), BF)
        gs[q, :, rim] = jnp.zeros((C, W), BF)
    pl.semaphore_wait(barrier, everyone - 1)

    from_row = cols(other * (H - 1), 1)
    to_row = rim
    halo_copies = []
    for d in range(nchan):
        there = lax.rem(chan + d, nchan)
        halo_copies.append(
            copy(x_ref.at[:, from_row], xs.at[1, mine, to_row], row_sem, (d,), at(lon, there, other))
        )
        for side in range(2):
            lon_to = lax.rem(lon + (nlon - 1 if side == 0 else 1), nlon)
            for dl in range(2):
                halo_copies.append(
                    copy(
                        edge.at[pl.ds(side * H, H)],
                        hx.at[chan, pl.ds(((1 - side) * 2 + dl) * H, H)],
                        col_sem, (d, side, dl),
                        at(lon_to, there, lat if dl == 0 else other),
                    )
                )
    for c in halo_copies:
        c.start()
    step = H // PIECES
    x_starts = [0] + [step * j + 1 for j in range(1, PIECES)] + [H]
    x_copies = []
    for j in range(PIECES):
        count = x_starts[j + 1] - x_starts[j]
        row = walk(x_starts[j], count)
        x_copies.append([
            copy(
                x_ref.at[:, cols(row, count)], xs.at[1, mine, cols(row + 1, count)],
                x_sem, (d, j), at(lon, lax.rem(chan + d, nchan), lat),
            )
            for d in range(1, nchan)
        ])
        for c in x_copies[j]:
            c.start()

    @pl.loop(0, H + 2)
    def _(r):
        k = lax.broadcasted_iota(jnp.int32, (W + 128, 2 * W), 0)
        n = lax.broadcasted_iota(jnp.int32, (W + 128, 2 * W), 1)
        first = jnp.where(lat == 1, 2 * H - 1, -1000)
        last = jnp.where(lat == 0, H, -1000)
        held = jnp.where(r == 0, first, jnp.where(r == H + 1, last, r - 1))
        right = n >= W
        col = jnp.where(right, n - W, n)
        want = jnp.where(right, col + 1, col - 1)
        want = jnp.where(right & (col == W - 1), W + 2 * H + held, want)
        want = jnp.where((~right) & (col == 0), W + held, want)
        hit = jnp.where(k == want, 1.0, 0.0).astype(BF)
        shift[:, pl.ds(pl.multiple_of(r * 2 * W, 2 * W), 2 * W)] = hit

    for t in range(9):
        w2[:, pl.ds(t * CA, CA)] = w_ref[pl.ds(t * C, C), :]
    wt[...] = jnp.transpose(w_ref[...].astype(F32)).astype(BF)

    def build_shifts(field, columns, start, count):
        @pl.loop(0, count)
        def _(i):
            r = start + i
            here = cols(r, 1)
            both = jnp.concatenate([field[1, :, here], columns], axis=1)
            moved = jnp.dot(
                both, shift[:, pl.ds(pl.multiple_of(r * 2 * W, 2 * W), 2 * W)],
                preferred_element_type=F32,
            ).astype(BF)
            field[0, :, here] = moved[:, :W]
            field[2, :, here] = moved[:, W:]

    def turned(blocks):
        have = sum(b.shape[0] for b in blocks)
        full = jnp.concatenate(blocks + [jnp.zeros((128 - have, C), BF)], axis=0)
        return jnp.transpose(full.astype(F32)).astype(BF)

    for c in halo_copies:
        c.wait()
    for k in range(nchan):
        hc[pl.ds(k * C, C), :] = turned([hx[k]])

    ring = nlon * nlat
    spot = lon * nlat + lat
    group_rows = 3 * C
    half = R // 2
    quarter = half // nlon
    base = pl.multiple_of(lat * half, half)
    far = pl.ds(pl.multiple_of(other * half, half), half)
    core_copies, bias_copies, dx_copies = [], [], []
    dx_starts = [0] + [step * j - 1 for j in range(1, PIECES)] + [H]
    if R > group_rows:
        for g in range(3):
            dwp[g, pl.ds(group_rows, R - group_rows), :] = jnp.zeros((R - group_rows, CA), F32)
    for j in range(PIECES):
        final = j == PIECES - 1
        for c in x_copies[j]:
            c.wait()
        if final:
            for c in dx_copies:
                c.start()
        count = x_starts[j + 1] - x_starts[j]
        if j == 0:
            build_shifts(xs, hc[...], jnp.where(lat == 1, 0, H + 1 - count), count + 1)
        else:
            build_shifts(xs, hc[...], walk(x_starts[j], count) + 1, count)
        row = walk(j * step, step)
        stack = jnp.concatenate(
            [xs[q, :, cols(row + p, step)] for p in range(3) for q in range(3)], axis=0
        )
        preact = jnp.dot(w2[...], stack, preferred_element_type=F32) + b_ref[...]
        upstream = ct_ref[:, cols(row, step)].astype(F32)
        grad = (upstream * gelu_slope(preact)).astype(BF)
        gs[1, :, cols(row + 1, step)] = grad
        gedge[j] = edges(grad, row)
        grad_copies = []
        if j == 0:
            grad_copies.append(
                copy(gs.at[1, :, cols(other * (H - 1) + 1, 1)], gs.at[1, :, to_row], grow_sem, (0,), at(lon, chan, other))
            )
        for side in range(2):
            lon_to = lax.rem(lon + (nlon - 1 if side == 0 else 1), nlon)
            tile = gedge.at[j, pl.ds(side * H, H)]
            grad_copies.append(copy(tile, hg.at[j, 1 - side], gcol_sem, (j, side), at(lon_to, chan, lat)))
            if j == 0:
                grad_copies.append(copy(tile, hgo.at[1 - side], gother_sem, (side,), at(lon_to, chan, other)))
        for c in grad_copies:
            c.start()
        if final:
            bias[spot] = nt(jnp.ones((8, L), BF), gs[1, :, pl.ds(W, L)])
            for d in range(1, ring):
                peer = lax.rem(spot + d, ring)
                c = copy(bias.at[spot], bias.at[spot], bias_sem, (d,), at(peer // nlat, chan, lax.rem(peer, nlat)))
                c.start()
                bias_copies.append(c)
        for p in range(3):
            for q in range(3):
                here = pl.ds(q * C, C)
                more = nt(grad, xs[q, :, cols(row + p, step)])
                dwp[p, here, :] = more if j == 0 else dwp[p, here, :] + more
            if final:
                dwsend[p] = dwp[p, far, :].astype(BF)
                c = copy(dwsend.at[p], dwcore.at[p], core_sem, (p,), at(lon, chan, other))
                c.start()
                core_copies.append(c)
        for c in grad_copies:
            c.wait()
        if j == 0:
            sides = turned([hg[j, 0], hgo[0], hg[j, 1], hgo[1]])
            build_shifts(gs, sides, jnp.where(lat == 1, 0, H + 1 - step), step + 1)
        else:
            blank = jnp.zeros((H, C), BF)
            sides = turned([hg[j, 0], blank, hg[j, 1], blank])
            build_shifts(gs, sides, row + 1, step)
        count = dx_starts[j + 1] - dx_starts[j]
        row = walk(dx_starts[j], count)
        stack = jnp.concatenate(
            [gs[2 - q, :, cols(row + 2 - p, count)] for p in range(3) for q in range(3)], axis=0
        )
        whole = jnp.dot(wt[...], stack, preferred_element_type=F32)
        dxf[:, cols(row, count)] = whole
        dxs[:, cols(row, count)] = whole.astype(BF)
        for d in range(1, nchan):
            there = lax.rem(chan + d, nchan)
            theirs = pl.ds(pl.multiple_of(there * C, C), C)
            c = copy(
                dxs.at[theirs, cols(row, count)], dxr.at[d, :, cols(row, count)],
                dx_sem, (d, j), at(lon, there, lat),
            )
            if final:
                c.start()
            dx_copies.append(c)

    rs_copies = []
    for g in range(3):
        core_copies[g].wait()
        summed = dwp[g, pl.ds(base, half), :] + dwcore[g].astype(F32)
        dwp[g, pl.ds(base, half), :] = summed
        zsend[g] = summed.astype(BF)
        rs_copies.append([])
        for d in range(1, nlon):
            there = lax.rem(lon + d, nlon)
            c = copy(
                zsend.at[g, pl.ds(pl.multiple_of(there * quarter, 16), quarter), :],
                zrecv.at[g, d], rs_sem, (g, d), at(there, chan, lat),
            )
            c.start()
            rs_copies[g].append(c)
    own_rows = pl.ds(pl.multiple_of(base + lon * quarter, 16), quarter)
    ag_copies, fwd_copies = [], []
    for g in range(3):
        total = dwp[g, own_rows, :]
        for d in range(1, nlon):
            rs_copies[g][d - 1].wait()
            total = total + zrecv[g, d].astype(F32)
        gathered[g, own_rows, :] = total.astype(BF)
        ag_copies.append([])
        for d in range(1, nlon):
            c = copy(
                gathered.at[g, own_rows, :], gathered.at[g, own_rows, :], ag_sem, (g, d),
                at(lax.rem(lon + d, nlon), chan, lat),
            )
            c.start()
            ag_copies[g].append(c)

    def finish_dx(j):
        count = dx_starts[j + 1] - dx_starts[j]
        here = cols(walk(dx_starts[j], count), count)
        acc = dxf[mine, here]
        for d in range(1, nchan):
            dx_copies[j * (nchan - 1) + d - 1].wait()
            acc = acc + dxr[d, :, here].astype(F32)
        dx_ref[:, here] = acc.astype(BF)

    for j in range(PIECES - 1):
        finish_dx(j)
    for g in range(3):
        for d in range(nlon):
            if d > 0:
                ag_copies[g][d - 1].wait()
            source = lax.rem(lon + nlon - d, nlon)
            rows = pl.ds(pl.multiple_of(base + source * quarter, 16), quarter)
            c = copy(gathered.at[g, rows, :], gathered.at[g, rows, :], fwd_sem, (g, d), at(lon, chan, other))
            c.start()
            fwd_copies.append(c)
    finish_dx(PIECES - 1)
    for c in bias_copies:
        c.wait()
    db_ref[...] = jnp.sum(bias[...], axis=0)
    for c in fwd_copies:
        c.wait()
    dw_ref[...] = gathered[...]


def local(nlon, nchan, nlat, inputs, cotangent, weight, bias_vector):
    C, H, W = inputs.shape
    CA = weight.shape[3]
    L = H * W
    step = nlat * nlon * 16
    R = -(-3 * C // step) * step
    half = R // nlat
    sizes = (nlon, nchan, nlat, C, CA, H, W, R)
    wide = (H + 2) * W
    vmem = pl.BlockSpec(memory_space=pltpu.VMEM)
    dma = pltpu.SemaphoreType.DMA
    dx, dw, db = pl.pallas_call(
        functools.partial(kernel, sizes),
        out_shape=(
            jax.ShapeDtypeStruct((C, L), BF),
            jax.ShapeDtypeStruct((3, R, CA), BF),
            jax.ShapeDtypeStruct((8, C), F32),
        ),
        in_specs=[vmem] * 4,
        out_specs=(vmem,) * 3,
        scratch_shapes=[
            pltpu.VMEM((3, CA, wide), BF),
            pltpu.VMEM((nchan, 4 * H, C), BF),
            pltpu.VMEM((CA, 128), BF),
            pltpu.VMEM((2 * H, C), BF),
            pltpu.VMEM((W + 128, (H + 2) * 2 * W), BF),
            pltpu.VMEM((C, 9 * CA), BF),
            pltpu.VMEM((CA, 9 * C), BF),
            pltpu.VMEM((3, C, wide), BF),
            pltpu.VMEM((PIECES, 2, H, C), BF),
            pltpu.VMEM((2, H, C), BF),
            pltpu.VMEM((PIECES, 2 * H, C), BF),
            pltpu.VMEM((3, R, CA), F32),
            pltpu.VMEM((3, half, CA), BF),
            pltpu.VMEM((3, half, CA), BF),
            pltpu.VMEM((3, half, CA), BF),
            pltpu.VMEM((3, nlon, half // nlon, CA), BF),
            pltpu.VMEM((3, R, CA), BF),
            pltpu.VMEM((nlon * nlat, 8, C), F32),
            pltpu.VMEM((CA, L), F32),
            pltpu.VMEM((CA, L), BF),
            pltpu.VMEM((nchan, C, L), BF),
            dma((2, nchan, PIECES)),
            dma((2, nchan)),
            dma((2, nchan, 2, 2)),
            dma((2, 1)),
            dma((2, PIECES, 2)),
            dma((2, 2)),
            dma((2, 3)),
            dma((2, 3, nlon)),
            dma((2, 3, nlon)),
            dma((2, 3, nlon)),
            dma((2, nlon * nlat)),
            dma((2, nchan, PIECES)),
        ],
        compiler_params=pltpu.CompilerParams(
            collective_id=0, has_side_effects=True, vmem_limit_bytes=48 * 1024 * 1024
        ),
        cost_estimate=pl.CostEstimate(
            flops=3 * 2 * 9 * C * CA * L, bytes_accessed=4 * C * L * 2, transcendentals=2 * C * L
        ),
        name="conv_backward",
    )(
        inputs.reshape(C, L),
        cotangent.reshape(C, L),
        weight.reshape(9 * C, CA),
        bias_vector.reshape(C, 1),
    )
    weight_grad = dw[:, : 3 * C].astype(F32).reshape(3, 3, C, CA)
    return dx.reshape(C, H, W), weight_grad, db[0]


def solution(mesh):
    shape = mesh.shape
    placed = (
        P("chan", ("groups", "lat"), "lon"),
        P("chan", ("groups", "lat"), "lon"),
        P(None, None, "chan", None),
        P("chan"),
    )
    return jax.shard_map(
        functools.partial(local, shape["lon"], shape["chan"], shape["lat"]),
        mesh=mesh,
        in_specs=placed,
        out_specs=(
            P("chan", ("groups", "lat"), "lon"),
            P("groups", None, "chan", None),
            P(("groups", "chan")),
        ),
        check_vma=False,
    )
```

```python
import functools

import jax
import jax.numpy as jnp
from jax import lax
from jax.experimental import pallas as pl
from jax.experimental.pallas import tpu as pltpu
from jax.sharding import PartitionSpec as P

MESH = pl.DeviceIdType.MESH
BF = jnp.bfloat16
F32 = jnp.float32
PIECES = 4


def gelu_slope(preact):
    normal_cdf = 0.5 * (1.0 + lax.erf(preact * 0.7071067811865476))
    density = jnp.exp(-0.5 * preact * preact) * 0.3989422804014327
    return normal_cdf + preact * density


def nt(a, b):
    return lax.dot_general(a, b, (((1,), (1,)), ((), ())), preferred_element_type=F32)


def kernel(
    sizes,
    x_ref, ct_ref, w_ref, b_ref,
    dx_ref, dw_ref, db_ref,
    xs, hx, hc, edge, w2, wt, gs, hg, hgo, gedge,
    dwp, dwsend, dwcore, zsend, zrecv, gathered, bias, dxf, dxs, dxr,
    x_sem, row_sem, col_sem, grow_sem, gcol_sem, gother_sem, core_sem, rs_sem, ag_sem, fwd_sem, bias_sem, dx_sem,
):
    nlon, nchan, nlat, C, CA, H, W, R = sizes
    L = H * W
    group = lax.axis_index("groups")
    lon = lax.axis_index("lon")
    chan = lax.axis_index("chan")
    lat = lax.axis_index("lat")
    other = 1 - lat

    def at(a, b, c):
        return (group, a, b, c)

    def copy(src, dst, sems, index, device):
        return pltpu.make_async_remote_copy(
            src_ref=src, dst_ref=dst,
            send_sem=sems.at[(0,) + index], recv_sem=sems.at[(1,) + index],
            device_id=device, device_id_type=MESH,
        )

    everyone = nlon * nchan * nlat
    me = (lon * nchan + chan) * nlat + lat
    barrier = pltpu.get_barrier_semaphore()

    @pl.loop(1, everyone)
    def _(d):
        peer = lax.rem(me + d, everyone)
        pl.semaphore_signal(
            barrier, inc=1, device_id_type=MESH,
            device_id=at(peer // (nchan * nlat), lax.rem(peer // nlat, nchan), lax.rem(peer, nlat)),
        )

    def edges(field, start):
        rows, lanes = 2 * H, field.shape[1]
        row = lax.broadcasted_iota(jnp.int32, (rows, lanes), 0)
        lane = lax.broadcasted_iota(jnp.int32, (rows, lanes), 1) + start * W
        want = jnp.where(row < H, row * W, (row - H) * W + W - 1)
        pick = jnp.where(lane == want, 1.0, 0.0).astype(BF)
        return nt(pick, field).astype(BF)

    def walk(start, count):
        return jnp.where(lat == 1, start, H - start - count)

    def cols(row, count):
        return pl.ds(pl.multiple_of(row * W, W), count * W)

    edge[...] = edges(x_ref[...], 0)
    mine = pl.ds(pl.multiple_of(chan * C, C), C)
    xs[1, mine, pl.ds(W, L)] = x_ref[...]
    rim = cols(lat * (H + 1), 1)
    for q in range(3):
        xs[q, :, rim] = jnp.zeros((CA, W), BF)
        gs[q, :, rim] = jnp.zeros((C, W), BF)
    pl.semaphore_wait(barrier, everyone - 1)

    from_row = cols(other * (H - 1), 1)
    to_row = rim
    halo_copies = []
    for d in range(nchan):
        there = lax.rem(chan + d, nchan)
        halo_copies.append(
            copy(x_ref.at[:, from_row], xs.at[1, mine, to_row], row_sem, (d,), at(lon, there, other))
        )
        for side in range(2):
            lon_to = lax.rem(lon + (nlon - 1 if side == 0 else 1), nlon)
            for dl in range(2):
                halo_copies.append(
                    copy(
                        edge.at[pl.ds(side * H, H)],
                        hx.at[chan, pl.ds(((1 - side) * 2 + dl) * H, H)],
                        col_sem, (d, side, dl),
                        at(lon_to, there, lat if dl == 0 else other),
                    )
                )
    for c in halo_copies:
        c.start()
    step = H // PIECES
    x_starts = [0] + [step * j + 1 for j in range(1, PIECES)] + [H]
    x_copies = []
    for j in range(PIECES):
        count = x_starts[j + 1] - x_starts[j]
        row = walk(x_starts[j], count)
        x_copies.append([
            copy(
                x_ref.at[:, cols(row, count)], xs.at[1, mine, cols(row + 1, count)],
                x_sem, (d, j), at(lon, lax.rem(chan + d, nchan), lat),
            )
            for d in range(1, nchan)
        ])
        for c in x_copies[j]:
            c.start()

    for t in range(9):
        w2[:, pl.ds(t * CA, CA)] = w_ref[pl.ds(t * C, C), :]
    wt[...] = jnp.transpose(w_ref[...])
    bias_col = jnp.transpose(jnp.broadcast_to(b_ref[...], (128, C)))[:, :1]

    def build_shifts(field, columns, start, count):
        lane = lax.broadcasted_iota(jnp.int32, columns.shape, 1)
        for i in range(count):
            r = start + i
            here = cols(r, 1)
            held = jnp.where(r == 0, 2 * H - 1, jnp.where(r == H + 1, H, r - 1))
            row = field[1, :, here]
            left = pltpu.roll(columns, lax.rem(W - held, W), 1)
            right = pltpu.roll(columns, lax.rem(2 * W - 1 - 2 * H - held, W), 1)
            field[0, :, here] = jnp.where(lane == 0, left, pltpu.roll(row, 1, 1))
            field[2, :, here] = jnp.where(lane == W - 1, right, pltpu.roll(row, W - 1, 1))

    def turned(blocks):
        have = sum(b.shape[0] for b in blocks)
        full = jnp.concatenate(blocks + [jnp.zeros((128 - have, C), BF)], axis=0)
        return jnp.transpose(full)

    for c in halo_copies:
        c.wait()
    for k in range(nchan):
        hc[pl.ds(k * C, C), :] = turned([hx[k]])

    ring = nlon * nlat
    spot = lon * nlat + lat
    group_rows = 3 * C
    half = R // 2
    quarter = half // nlon
    base = pl.multiple_of(lat * half, half)
    far = pl.ds(pl.multiple_of(other * half, half), half)
    core_copies, bias_copies, dx_copies = [], [], []
    dx_starts = [0] + [step * j - 1 for j in range(1, PIECES)] + [H]
    if R > group_rows:
        for g in range(3):
            dwp[g, pl.ds(group_rows, R - group_rows), :] = jnp.zeros((R - group_rows, CA), F32)
    for j in range(PIECES):
        final = j == PIECES - 1
        for c in x_copies[j]:
            c.wait()
        if final:
            for c in dx_copies:
                c.start()
        count = x_starts[j + 1] - x_starts[j]
        if j == 0:
            build_shifts(xs, hc[...], jnp.where(lat == 1, 0, H + 1 - count), count + 1)
        else:
            build_shifts(xs, hc[...], walk(x_starts[j], count) + 1, count)
        row = walk(j * step, step)
        stack = jnp.concatenate(
            [xs[q, :, cols(row + p, step)] for p in range(3) for q in range(3)], axis=0
        )
        preact = jnp.dot(w2[...], stack, preferred_element_type=F32) + bias_col
        upstream = ct_ref[:, cols(row, step)].astype(F32)
        grad = (upstream * gelu_slope(preact)).astype(BF)
        gs[1, :, cols(row + 1, step)] = grad
        gedge[j] = edges(grad, row)
        grad_copies = []
        if j == 0:
            grad_copies.append(
                copy(gs.at[1, :, cols(other * (H - 1) + 1, 1)], gs.at[1, :, to_row], grow_sem, (0,), at(lon, chan, other))
            )
        for side in range(2):
            lon_to = lax.rem(lon + (nlon - 1 if side == 0 else 1), nlon)
            tile = gedge.at[j, pl.ds(side * H, H)]
            grad_copies.append(copy(tile, hg.at[j, 1 - side], gcol_sem, (j, side), at(lon_to, chan, lat)))
            if j == 0:
                grad_copies.append(copy(tile, hgo.at[1 - side], gother_sem, (side,), at(lon_to, chan, other)))
        for c in grad_copies:
            c.start()
        if final:
            bias[spot] = nt(jnp.ones((8, L), BF), gs[1, :, pl.ds(W, L)])
            for d in range(1, ring):
                peer = lax.rem(spot + d, ring)
                c = copy(bias.at[spot], bias.at[spot], bias_sem, (d,), at(peer // nlat, chan, lax.rem(peer, nlat)))
                c.start()
                bias_copies.append(c)
        for p in range(3):
            for q in range(3):
                here = pl.ds(q * C, C)
                more = nt(grad, xs[q, :, cols(row + p, step)])
                dwp[p, here, :] = more if j == 0 else dwp[p, here, :] + more
            if final:
                dwsend[p] = dwp[p, far, :].astype(BF)
                c = copy(dwsend.at[p], dwcore.at[p], core_sem, (p,), at(lon, chan, other))
                c.start()
                core_copies.append(c)
        for c in grad_copies:
            c.wait()
        if j == 0:
            sides = turned([hg[j, 0], hgo[0], hg[j, 1], hgo[1]])
            build_shifts(gs, sides, jnp.where(lat == 1, 0, H + 1 - step), step + 1)
        else:
            blank = jnp.zeros((H, C), BF)
            sides = turned([hg[j, 0], blank, hg[j, 1], blank])
            build_shifts(gs, sides, row + 1, step)
        count = dx_starts[j + 1] - dx_starts[j]
        row = walk(dx_starts[j], count)
        stack = jnp.concatenate(
            [gs[2 - q, :, cols(row + 2 - p, count)] for p in range(3) for q in range(3)], axis=0
        )
        whole = jnp.dot(wt[...], stack, preferred_element_type=F32)
        dxf[:, cols(row, count)] = whole
        dxs[:, cols(row, count)] = whole.astype(BF)
        for d in range(1, nchan):
            there = lax.rem(chan + d, nchan)
            theirs = pl.ds(pl.multiple_of(there * C, C), C)
            c = copy(
                dxs.at[theirs, cols(row, count)], dxr.at[d, :, cols(row, count)],
                dx_sem, (d, j), at(lon, there, lat),
            )
            if final:
                c.start()
            dx_copies.append(c)

    rs_copies = []
    for g in range(3):
        core_copies[g].wait()
        summed = dwp[g, pl.ds(base, half), :] + dwcore[g].astype(F32)
        dwp[g, pl.ds(base, half), :] = summed
        zsend[g] = summed.astype(BF)
        rs_copies.append([])
        for d in range(1, nlon):
            there = lax.rem(lon + d, nlon)
            c = copy(
                zsend.at[g, pl.ds(pl.multiple_of(there * quarter, 16), quarter), :],
                zrecv.at[g, d], rs_sem, (g, d), at(there, chan, lat),
            )
            c.start()
            rs_copies[g].append(c)
    own_rows = pl.ds(pl.multiple_of(base + lon * quarter, 16), quarter)
    ag_copies, fwd_copies = [], []
    for g in range(3):
        total = dwp[g, own_rows, :]
        for d in range(1, nlon):
            rs_copies[g][d - 1].wait()
            total = total + zrecv[g, d].astype(F32)
        gathered[g, own_rows, :] = total.astype(BF)
        ag_copies.append([])
        for d in range(1, nlon):
            c = copy(
                gathered.at[g, own_rows, :], gathered.at[g, own_rows, :], ag_sem, (g, d),
                at(lax.rem(lon + d, nlon), chan, lat),
            )
            c.start()
            ag_copies[g].append(c)

    def finish_dx(j):
        count = dx_starts[j + 1] - dx_starts[j]
        here = cols(walk(dx_starts[j], count), count)
        acc = dxf[mine, here]
        for d in range(1, nchan):
            dx_copies[j * (nchan - 1) + d - 1].wait()
            acc = acc + dxr[d, :, here].astype(F32)
        dx_ref[:, here] = acc.astype(BF)

    for j in range(PIECES - 1):
        finish_dx(j)
    for g in range(3):
        for d in range(nlon):
            if d > 0:
                ag_copies[g][d - 1].wait()
            source = lax.rem(lon + nlon - d, nlon)
            rows = pl.ds(pl.multiple_of(base + source * quarter, 16), quarter)
            c = copy(gathered.at[g, rows, :], gathered.at[g, rows, :], fwd_sem, (g, d), at(lon, chan, other))
            c.start()
            fwd_copies.append(c)
    finish_dx(PIECES - 1)
    for c in bias_copies:
        c.wait()
    db_ref[...] = jnp.sum(bias[...], axis=0)[:1]
    for c in fwd_copies:
        c.wait()
    dw_ref[...] = gathered[...]


def local(nlon, nchan, nlat, inputs, cotangent, weight, bias_vector):
    C, H, W = inputs.shape
    CA = weight.shape[3]
    L = H * W
    step = nlat * nlon * 16
    R = -(-3 * C // step) * step
    half = R // nlat
    sizes = (nlon, nchan, nlat, C, CA, H, W, R)
    wide = (H + 2) * W
    vmem = pl.BlockSpec(memory_space=pltpu.VMEM)
    dma = pltpu.SemaphoreType.DMA
    dx, dw, db = pl.pallas_call(
        functools.partial(kernel, sizes),
        out_shape=(
            jax.ShapeDtypeStruct((C, L), BF),
            jax.ShapeDtypeStruct((3, R, CA), BF),
            jax.ShapeDtypeStruct((1, C), F32),
        ),
        in_specs=[vmem] * 4,
        out_specs=(vmem,) * 3,
        scratch_shapes=[
            pltpu.VMEM((3, CA, wide), BF),
            pltpu.VMEM((nchan, 4 * H, C), BF),
            pltpu.VMEM((CA, 128), BF),
            pltpu.VMEM((2 * H, C), BF),
            pltpu.VMEM((C, 9 * CA), BF),
            pltpu.VMEM((CA, 9 * C), BF),
            pltpu.VMEM((3, C, wide), BF),
            pltpu.VMEM((PIECES, 2, H, C), BF),
            pltpu.VMEM((2, H, C), BF),
            pltpu.VMEM((PIECES, 2 * H, C), BF),
            pltpu.VMEM((3, R, CA), F32),
            pltpu.VMEM((3, half, CA), BF),
            pltpu.VMEM((3, half, CA), BF),
            pltpu.VMEM((3, half, CA), BF),
            pltpu.VMEM((3, nlon, half // nlon, CA), BF),
            pltpu.VMEM((3, R, CA), BF),
            pltpu.VMEM((nlon * nlat, 8, C), F32),
            pltpu.VMEM((CA, L), F32),
            pltpu.VMEM((CA, L), BF),
            pltpu.VMEM((nchan, C, L), BF),
            dma((2, nchan, PIECES)),
            dma((2, nchan)),
            dma((2, nchan, 2, 2)),
            dma((2, 1)),
            dma((2, PIECES, 2)),
            dma((2, 2)),
            dma((2, 3)),
            dma((2, 3, nlon)),
            dma((2, 3, nlon)),
            dma((2, 3, nlon)),
            dma((2, nlon * nlat)),
            dma((2, nchan, PIECES)),
        ],
        compiler_params=pltpu.CompilerParams(
            collective_id=0, has_side_effects=True, vmem_limit_bytes=48 * 1024 * 1024
        ),
        cost_estimate=pl.CostEstimate(
            flops=3 * 2 * 9 * C * CA * L, bytes_accessed=4 * C * L * 2, transcendentals=2 * C * L
        ),
        name="conv_backward",
    )(
        inputs.reshape(C, L),
        cotangent.reshape(C, L),
        weight.reshape(9 * C, CA),
        bias_vector.reshape(1, C),
    )
    weight_grad = dw[:, : 3 * C].astype(F32).reshape(3, 3, C, CA)
    return dx.reshape(C, H, W), weight_grad, db.reshape(C)


def solution(mesh):
    shape = mesh.shape
    placed = (
        P("chan", ("groups", "lat"), "lon"),
        P("chan", ("groups", "lat"), "lon"),
        P(None, None, "chan", None),
        P("chan"),
    )
    return jax.shard_map(
        functools.partial(local, shape["lon"], shape["chan"], shape["lat"]),
        mesh=mesh,
        in_specs=placed,
        out_specs=(
            P("chan", ("groups", "lat"), "lon"),
            P("groups", None, "chan", None),
            P(("groups", "chan")),
        ),
        check_vma=False,
    )
```

```python
import functools

import jax
import jax.numpy as jnp
from jax import lax
from jax.experimental import pallas as pl
from jax.experimental.pallas import tpu as pltpu
from jax.sharding import PartitionSpec as P

MESH = pl.DeviceIdType.MESH
BF = jnp.bfloat16
F32 = jnp.float32
PIECES = 4


def gelu_slope(preact):
    normal_cdf = 0.5 * (1.0 + lax.erf(preact * 0.7071067811865476))
    density = jnp.exp(-0.5 * preact * preact) * 0.3989422804014327
    return normal_cdf + preact * density


def nt(a, b):
    return lax.dot_general(a, b, (((1,), (1,)), ((), ())), preferred_element_type=F32)


def kernel(
    sizes,
    x_ref, ct_ref, w_ref, b_ref,
    dx_ref, dw_ref, db_ref,
    xs, hx, hc, edge, w2, wt, gs, hg, hgo, gedge,
    dwp, dwsend, dwcore, zsend, zrecv, gathered, bias, dxf, dxs, dxr,
    x_sem, row_sem, col_sem, grow_sem, gcol_sem, gother_sem, core_sem, rs_sem, ag_sem, fwd_sem, bias_sem, dx_sem,
):
    nlon, nchan, nlat, C, CA, H, W, R = sizes
    L = H * W
    group = lax.axis_index("groups")
    lon = lax.axis_index("lon")
    chan = lax.axis_index("chan")
    lat = lax.axis_index("lat")
    other = 1 - lat

    def at(a, b, c):
        return (group, a, b, c)

    def copy(src, dst, sems, index, device):
        return pltpu.make_async_remote_copy(
            src_ref=src, dst_ref=dst,
            send_sem=sems.at[(0,) + index], recv_sem=sems.at[(1,) + index],
            device_id=device, device_id_type=MESH,
        )

    everyone = nlon * nchan * nlat
    me = (lon * nchan + chan) * nlat + lat
    barrier = pltpu.get_barrier_semaphore()

    @pl.loop(1, everyone)
    def _(d):
        peer = lax.rem(me + d, everyone)
        pl.semaphore_signal(
            barrier, inc=1, device_id_type=MESH,
            device_id=at(peer // (nchan * nlat), lax.rem(peer // nlat, nchan), lax.rem(peer, nlat)),
        )

    def edges(field, start):
        rows, lanes = 2 * H, field.shape[1]
        row = lax.broadcasted_iota(jnp.int32, (rows, lanes), 0)
        lane = lax.broadcasted_iota(jnp.int32, (rows, lanes), 1) + start * W
        want = jnp.where(row < H, row * W, (row - H) * W + W - 1)
        pick = jnp.where(lane == want, 1.0, 0.0).astype(BF)
        return nt(pick, field).astype(BF)

    def walk(start, count):
        return jnp.where(lat == 1, start, H - start - count)

    def cols(row, count):
        return pl.ds(pl.multiple_of(row * W, W), count * W)

    edge[...] = edges(x_ref[...], 0)
    mine = pl.ds(pl.multiple_of(chan * C, C), C)
    xs[1, mine, pl.ds(W, L)] = x_ref[...]
    rim = cols(lat * (H + 1), 1)
    for q in range(3):
        xs[q, :, rim] = jnp.zeros((CA, W), BF)
        gs[q, :, rim] = jnp.zeros((C, W), BF)
    pl.semaphore_wait(barrier, everyone - 1)

    from_row = cols(other * (H - 1), 1)
    to_row = rim
    halo_copies = []
    for d in range(nchan):
        there = lax.rem(chan + d, nchan)
        halo_copies.append(
            copy(x_ref.at[:, from_row], xs.at[1, mine, to_row], row_sem, (d,), at(lon, there, other))
        )
        for side in range(2):
            lon_to = lax.rem(lon + (nlon - 1 if side == 0 else 1), nlon)
            for dl in range(2):
                halo_copies.append(
                    copy(
                        edge.at[pl.ds(side * H, H)],
                        hx.at[chan, pl.ds(((1 - side) * 2 + dl) * H, H)],
                        col_sem, (d, side, dl),
                        at(lon_to, there, lat if dl == 0 else other),
                    )
                )
    for c in halo_copies:
        c.start()
    step = H // PIECES
    x_starts = [0] + [step * j + 1 for j in range(1, PIECES)] + [H]
    x_copies = []
    for j in range(PIECES):
        count = x_starts[j + 1] - x_starts[j]
        row = walk(x_starts[j], count)
        x_copies.append([
            copy(
                x_ref.at[:, cols(row, count)], xs.at[1, mine, cols(row + 1, count)],
                x_sem, (d, j), at(lon, lax.rem(chan + d, nchan), lat),
            )
            for d in range(1, nchan)
        ])
        for c in x_copies[j]:
            c.start()

    for t in range(9):
        w2[:, pl.ds(t * CA, CA)] = w_ref[pl.ds(t * C, C), :]
    wt[...] = jnp.transpose(w_ref[...])
    bias_col = jnp.transpose(jnp.broadcast_to(b_ref[...], (128, C)))[:, :1]

    def build_shifts(field, columns, start, count):
        lane = lax.broadcasted_iota(jnp.int32, columns.shape, 1)
        for i in range(count):
            r = start + i
            here = cols(r, 1)
            held = jnp.where(r == 0, 2 * H - 1, jnp.where(r == H + 1, H, r - 1))
            row = field[1, :, here]
            left = pltpu.roll(columns, lax.rem(W - held, W), 1)
            right = pltpu.roll(columns, lax.rem(2 * W - 1 - 2 * H - held, W), 1)
            field[0, :, here] = jnp.where(lane == 0, left, pltpu.roll(row, 1, 1))
            field[2, :, here] = jnp.where(lane == W - 1, right, pltpu.roll(row, W - 1, 1))

    def turned(blocks):
        have = sum(b.shape[0] for b in blocks)
        full = jnp.concatenate(blocks + [jnp.zeros((128 - have, C), BF)], axis=0)
        return jnp.transpose(full)

    for c in halo_copies:
        c.wait()
    for k in range(nchan):
        hc[pl.ds(k * C, C), :] = turned([hx[k]])

    ring = nlon * nlat
    spot = lon * nlat + lat
    group_rows = 3 * C
    half = R // 2
    quarter = half // nlon
    base = pl.multiple_of(lat * half, half)
    far = pl.ds(pl.multiple_of(other * half, half), half)
    core_copies, bias_copies, dx_copies = [], [], []
    dx_starts = [0] + [step * j - 1 for j in range(1, PIECES)] + [H]
    if R > group_rows:
        for g in range(3):
            dwp[g, pl.ds(group_rows, R - group_rows), :] = jnp.zeros((R - group_rows, CA), F32)
    pending = []

    def input_grad(j, send):
        grad_copies, row = pending[j]
        for c in grad_copies:
            c.wait()
        if j == 0:
            sides = turned([hg[j, 0], hgo[0], hg[j, 1], hgo[1]])
            build_shifts(gs, sides, jnp.where(lat == 1, 0, H + 1 - step), step + 1)
        else:
            blank = jnp.zeros((H, C), BF)
            sides = turned([hg[j, 0], blank, hg[j, 1], blank])
            build_shifts(gs, sides, row + 1, step)
        count = dx_starts[j + 1] - dx_starts[j]
        row = walk(dx_starts[j], count)
        stack = jnp.concatenate(
            [gs[2 - q, :, cols(row + 2 - p, count)] for p in range(3) for q in range(3)], axis=0
        )
        whole = jnp.dot(wt[...], stack, preferred_element_type=F32)
        dxf[:, cols(row, count)] = whole
        dxs[:, cols(row, count)] = whole.astype(BF)
        for d in range(1, nchan):
            there = lax.rem(chan + d, nchan)
            theirs = pl.ds(pl.multiple_of(there * C, C), C)
            c = copy(
                dxs.at[theirs, cols(row, count)], dxr.at[d, :, cols(row, count)],
                dx_sem, (d, j), at(lon, there, lat),
            )
            if send:
                c.start()
            dx_copies.append(c)

    for j in range(PIECES):
        final = j == PIECES - 1
        for c in x_copies[j]:
            c.wait()
        if final:
            for c in dx_copies:
                c.start()
        count = x_starts[j + 1] - x_starts[j]
        if j == 0:
            build_shifts(xs, hc[...], jnp.where(lat == 1, 0, H + 1 - count), count + 1)
        else:
            build_shifts(xs, hc[...], walk(x_starts[j], count) + 1, count)
        row = walk(j * step, step)
        stack = jnp.concatenate(
            [xs[q, :, cols(row + p, step)] for p in range(3) for q in range(3)], axis=0
        )
        preact = jnp.dot(w2[...], stack, preferred_element_type=F32) + bias_col
        upstream = ct_ref[:, cols(row, step)].astype(F32)
        grad = (upstream * gelu_slope(preact)).astype(BF)
        gs[1, :, cols(row + 1, step)] = grad
        gedge[j] = edges(grad, row)
        grad_copies = []
        if j == 0:
            grad_copies.append(
                copy(gs.at[1, :, cols(other * (H - 1) + 1, 1)], gs.at[1, :, to_row], grow_sem, (0,), at(lon, chan, other))
            )
        for side in range(2):
            lon_to = lax.rem(lon + (nlon - 1 if side == 0 else 1), nlon)
            tile = gedge.at[j, pl.ds(side * H, H)]
            grad_copies.append(copy(tile, hg.at[j, 1 - side], gcol_sem, (j, side), at(lon_to, chan, lat)))
            if j == 0:
                grad_copies.append(copy(tile, hgo.at[1 - side], gother_sem, (side,), at(lon_to, chan, other)))
        for c in grad_copies:
            c.start()
        for p in range(3):
            for q in range(3):
                here = pl.ds(q * C, C)
                more = nt(grad, xs[q, :, cols(row + p, step)])
                dwp[p, here, :] = more if j == 0 else dwp[p, here, :] + more
            if final:
                dwsend[p] = dwp[p, far, :].astype(BF)
                c = copy(dwsend.at[p], dwcore.at[p], core_sem, (p,), at(lon, chan, other))
                c.start()
                core_copies.append(c)
        pending.append((grad_copies, row))
        if j > 0:
            input_grad(j - 1, final)

    rs_copies = []
    for g in range(3):
        core_copies[g].wait()
        summed = dwp[g, pl.ds(base, half), :] + dwcore[g].astype(F32)
        dwp[g, pl.ds(base, half), :] = summed
        zsend[g] = summed.astype(BF)
        rs_copies.append([])
        for d in range(1, nlon):
            there = lax.rem(lon + d, nlon)
            c = copy(
                zsend.at[g, pl.ds(pl.multiple_of(there * quarter, 16), quarter), :],
                zrecv.at[g, d], rs_sem, (g, d), at(there, chan, lat),
            )
            c.start()
            rs_copies[g].append(c)
    input_grad(PIECES - 1, True)
    bias[spot] = nt(jnp.ones((8, L), BF), gs[1, :, pl.ds(W, L)])
    for d in range(1, ring):
        peer = lax.rem(spot + d, ring)
        c = copy(bias.at[spot], bias.at[spot], bias_sem, (d,), at(peer // nlat, chan, lax.rem(peer, nlat)))
        c.start()
        bias_copies.append(c)
    own_rows = pl.ds(pl.multiple_of(base + lon * quarter, 16), quarter)
    ag_copies, fwd_copies = [], []
    for g in range(3):
        total = dwp[g, own_rows, :]
        for d in range(1, nlon):
            rs_copies[g][d - 1].wait()
            total = total + zrecv[g, d].astype(F32)
        gathered[g, own_rows, :] = total.astype(BF)
        ag_copies.append([])
        for d in range(1, nlon):
            c = copy(
                gathered.at[g, own_rows, :], gathered.at[g, own_rows, :], ag_sem, (g, d),
                at(lax.rem(lon + d, nlon), chan, lat),
            )
            c.start()
            ag_copies[g].append(c)

    def finish_dx(j):
        count = dx_starts[j + 1] - dx_starts[j]
        here = cols(walk(dx_starts[j], count), count)
        acc = dxf[mine, here]
        for d in range(1, nchan):
            dx_copies[j * (nchan - 1) + d - 1].wait()
            acc = acc + dxr[d, :, here].astype(F32)
        dx_ref[:, here] = acc.astype(BF)

    for j in range(PIECES - 1):
        finish_dx(j)
    for g in range(3):
        for d in range(nlon):
            if d > 0:
                ag_copies[g][d - 1].wait()
            source = lax.rem(lon + nlon - d, nlon)
            rows = pl.ds(pl.multiple_of(base + source * quarter, 16), quarter)
            c = copy(gathered.at[g, rows, :], gathered.at[g, rows, :], fwd_sem, (g, d), at(lon, chan, other))
            c.start()
            fwd_copies.append(c)
    finish_dx(PIECES - 1)
    for c in bias_copies:
        c.wait()
    db_ref[...] = jnp.sum(bias[...], axis=0)[:1]
    for c in fwd_copies:
        c.wait()
    dw_ref[...] = gathered[...]


def local(nlon, nchan, nlat, inputs, cotangent, weight, bias_vector):
    C, H, W = inputs.shape
    CA = weight.shape[3]
    L = H * W
    step = nlat * nlon * 16
    R = -(-3 * C // step) * step
    half = R // nlat
    sizes = (nlon, nchan, nlat, C, CA, H, W, R)
    wide = (H + 2) * W
    vmem = pl.BlockSpec(memory_space=pltpu.VMEM)
    dma = pltpu.SemaphoreType.DMA
    dx, dw, db = pl.pallas_call(
        functools.partial(kernel, sizes),
        out_shape=(
            jax.ShapeDtypeStruct((C, L), BF),
            jax.ShapeDtypeStruct((3, R, CA), BF),
            jax.ShapeDtypeStruct((1, C), F32),
        ),
        in_specs=[vmem] * 4,
        out_specs=(vmem,) * 3,
        scratch_shapes=[
            pltpu.VMEM((3, CA, wide), BF),
            pltpu.VMEM((nchan, 4 * H, C), BF),
            pltpu.VMEM((CA, 128), BF),
            pltpu.VMEM((2 * H, C), BF),
            pltpu.VMEM((C, 9 * CA), BF),
            pltpu.VMEM((CA, 9 * C), BF),
            pltpu.VMEM((3, C, wide), BF),
            pltpu.VMEM((PIECES, 2, H, C), BF),
            pltpu.VMEM((2, H, C), BF),
            pltpu.VMEM((PIECES, 2 * H, C), BF),
            pltpu.VMEM((3, R, CA), F32),
            pltpu.VMEM((3, half, CA), BF),
            pltpu.VMEM((3, half, CA), BF),
            pltpu.VMEM((3, half, CA), BF),
            pltpu.VMEM((3, nlon, half // nlon, CA), BF),
            pltpu.VMEM((3, R, CA), BF),
            pltpu.VMEM((nlon * nlat, 8, C), F32),
            pltpu.VMEM((CA, L), F32),
            pltpu.VMEM((CA, L), BF),
            pltpu.VMEM((nchan, C, L), BF),
            dma((2, nchan, PIECES)),
            dma((2, nchan)),
            dma((2, nchan, 2, 2)),
            dma((2, 1)),
            dma((2, PIECES, 2)),
            dma((2, 2)),
            dma((2, 3)),
            dma((2, 3, nlon)),
            dma((2, 3, nlon)),
            dma((2, 3, nlon)),
            dma((2, nlon * nlat)),
            dma((2, nchan, PIECES)),
        ],
        compiler_params=pltpu.CompilerParams(
            collective_id=0, has_side_effects=True, vmem_limit_bytes=48 * 1024 * 1024
        ),
        cost_estimate=pl.CostEstimate(
            flops=3 * 2 * 9 * C * CA * L, bytes_accessed=4 * C * L * 2, transcendentals=2 * C * L
        ),
        name="conv_backward",
    )(
        inputs.reshape(C, L),
        cotangent.reshape(C, L),
        weight.reshape(9 * C, CA),
        bias_vector.reshape(1, C),
    )
    weight_grad = dw[:, : 3 * C].astype(F32).reshape(3, 3, C, CA)
    return dx.reshape(C, H, W), weight_grad, db.reshape(C)


def solution(mesh):
    shape = mesh.shape
    placed = (
        P("chan", ("groups", "lat"), "lon"),
        P("chan", ("groups", "lat"), "lon"),
        P(None, None, "chan", None),
        P("chan"),
    )
    return jax.shard_map(
        functools.partial(local, shape["lon"], shape["chan"], shape["lat"]),
        mesh=mesh,
        in_specs=placed,
        out_specs=(
            P("chan", ("groups", "lat"), "lon"),
            P("groups", None, "chan", None),
            P(("groups", "chan")),
        ),
        check_vma=False,
    )
```

```python
import functools

import jax
import jax.numpy as jnp
from jax import lax
from jax.experimental import pallas as pl
from jax.experimental.pallas import tpu as pltpu
from jax.sharding import PartitionSpec as P

MESH = pl.DeviceIdType.MESH
BF = jnp.bfloat16
F32 = jnp.float32
PIECES = 4


def gelu_slope(preact):
    normal_cdf = 0.5 * (1.0 + lax.erf(preact * 0.7071067811865476))
    density = jnp.exp(-0.5 * preact * preact) * 0.3989422804014327
    return normal_cdf + preact * density


def nt(a, b):
    return lax.dot_general(a, b, (((1,), (1,)), ((), ())), preferred_element_type=F32)


def kernel(
    sizes,
    x_ref, ct_ref, w_ref, b_ref,
    dx_ref, dw_ref, db_ref,
    xs, hx, hc, edge, w2, wt, gs, hg, hgo, gedge,
    dwp, dwsend, dwcore, zsend, zrecv, gathered, bias, dxf, dxs, dxr,
    x_sem, row_sem, col_sem, grow_sem, gcol_sem, gother_sem, core_sem, rs_sem, ag_sem, fwd_sem, bias_sem, dx_sem,
):
    nlon, nchan, nlat, C, CA, H, W, R = sizes
    L = H * W
    group = lax.axis_index("groups")
    lon = lax.axis_index("lon")
    chan = lax.axis_index("chan")
    lat = lax.axis_index("lat")
    other = 1 - lat

    def at(a, b, c):
        return (group, a, b, c)

    def copy(src, dst, sems, index, device):
        return pltpu.make_async_remote_copy(
            src_ref=src, dst_ref=dst,
            send_sem=sems.at[(0,) + index], recv_sem=sems.at[(1,) + index],
            device_id=device, device_id_type=MESH,
        )

    everyone = nlon * nchan * nlat
    me = (lon * nchan + chan) * nlat + lat
    barrier = pltpu.get_barrier_semaphore()

    @pl.loop(1, everyone)
    def _(d):
        peer = lax.rem(me + d, everyone)
        pl.semaphore_signal(
            barrier, inc=1, device_id_type=MESH,
            device_id=at(peer // (nchan * nlat), lax.rem(peer // nlat, nchan), lax.rem(peer, nlat)),
        )

    def edges(field, start):
        rows, lanes = 2 * H, field.shape[1]
        row = lax.broadcasted_iota(jnp.int32, (rows, lanes), 0)
        lane = lax.broadcasted_iota(jnp.int32, (rows, lanes), 1) + start * W
        want = jnp.where(row < H, row * W, (row - H) * W + W - 1)
        pick = jnp.where(lane == want, 1.0, 0.0).astype(BF)
        return nt(pick, field).astype(BF)

    def walk(start, count):
        return jnp.where(lat == 1, start, H - start - count)

    def cols(row, count):
        return pl.ds(pl.multiple_of(row * W, W), count * W)

    edge[...] = edges(x_ref[...], 0)
    mine = pl.ds(pl.multiple_of(chan * C, C), C)
    xs[1, mine, pl.ds(W, L)] = x_ref[...]
    rim = cols(lat * (H + 1), 1)
    for q in range(3):
        xs[q, :, rim] = jnp.zeros((CA, W), BF)
        gs[q, :, rim] = jnp.zeros((C, W), BF)
    pl.semaphore_wait(barrier, everyone - 1)

    from_row = cols(other * (H - 1), 1)
    to_row = rim
    halo_copies = []
    for d in range(nchan):
        there = lax.rem(chan + d, nchan)
        halo_copies.append(
            copy(x_ref.at[:, from_row], xs.at[1, mine, to_row], row_sem, (d,), at(lon, there, other))
        )
        for side in range(2):
            lon_to = lax.rem(lon + (nlon - 1 if side == 0 else 1), nlon)
            for dl in range(2):
                halo_copies.append(
                    copy(
                        edge.at[pl.ds(side * H, H)],
                        hx.at[chan, pl.ds(((1 - side) * 2 + dl) * H, H)],
                        col_sem, (d, side, dl),
                        at(lon_to, there, lat if dl == 0 else other),
                    )
                )
    for c in halo_copies:
        c.start()
    step = H // PIECES
    x_starts = [0] + [step * j + 1 for j in range(1, PIECES)] + [H]
    x_copies = []
    for j in range(PIECES):
        count = x_starts[j + 1] - x_starts[j]
        row = walk(x_starts[j], count)
        x_copies.append([
            copy(
                x_ref.at[:, cols(row, count)], xs.at[1, mine, cols(row + 1, count)],
                x_sem, (d, j), at(lon, lax.rem(chan + d, nchan), lat),
            )
            for d in range(1, nchan)
        ])
        for c in x_copies[j]:
            c.start()

    for t in range(9):
        w2[:, pl.ds(t * CA, CA)] = w_ref[pl.ds(t * C, C), :]
    wt[...] = jnp.transpose(w_ref[...])
    bias_col = jnp.transpose(jnp.broadcast_to(b_ref[...], (128, C)))[:, :1]

    def build_shifts(field, columns, start, count):
        lane = lax.broadcasted_iota(jnp.int32, columns.shape, 1)
        for i in range(count):
            r = start + i
            here = cols(r, 1)
            held = jnp.where(r == 0, 2 * H - 1, jnp.where(r == H + 1, H, r - 1))
            row = field[1, :, here]
            left = pltpu.roll(columns, lax.rem(W - held, W), 1)
            right = pltpu.roll(columns, lax.rem(2 * W - 1 - 2 * H - held, W), 1)
            field[0, :, here] = jnp.where(lane == 0, left, pltpu.roll(row, 1, 1))
            field[2, :, here] = jnp.where(lane == W - 1, right, pltpu.roll(row, W - 1, 1))

    def turned(blocks):
        have = sum(b.shape[0] for b in blocks)
        full = jnp.concatenate(blocks + [jnp.zeros((128 - have, C), BF)], axis=0)
        return jnp.transpose(full)

    for c in halo_copies:
        c.wait()
    for k in range(nchan):
        hc[pl.ds(k * C, C), :] = turned([hx[k]])

    ring = nlon * nlat
    spot = lon * nlat + lat
    group_rows = 3 * C
    half = R // 2
    quarter = half // nlon
    base = pl.multiple_of(lat * half, half)
    far = pl.ds(pl.multiple_of(other * half, half), half)
    core_copies, bias_copies, dx_copies = [], [], []
    dx_starts = [0] + [step * j - 1 for j in range(1, PIECES)] + [H]
    if R > group_rows:
        for g in range(3):
            dwp[g, pl.ds(group_rows, R - group_rows), :] = jnp.zeros((R - group_rows, CA), F32)
    pending = []

    def input_grad(j):
        grad_copies, row = pending[j]
        for c in grad_copies:
            c.wait()
        if j == 0:
            sides = turned([hg[j, 0], hgo[0], hg[j, 1], hgo[1]])
            build_shifts(gs, sides, jnp.where(lat == 1, 0, H + 1 - step), step + 1)
        else:
            blank = jnp.zeros((H, C), BF)
            sides = turned([hg[j, 0], blank, hg[j, 1], blank])
            build_shifts(gs, sides, row + 1, step)
        count = dx_starts[j + 1] - dx_starts[j]
        row = walk(dx_starts[j], count)
        stack = jnp.concatenate(
            [gs[2 - q, :, cols(row + 2 - p, count)] for p in range(3) for q in range(3)], axis=0
        )
        whole = jnp.dot(wt[...], stack, preferred_element_type=F32)
        dxf[:, cols(row, count)] = whole
        dxs[:, cols(row, count)] = whole.astype(BF)
        for d in range(1, nchan):
            there = lax.rem(chan + d, nchan)
            theirs = pl.ds(pl.multiple_of(there * C, C), C)
            c = copy(
                dxs.at[theirs, cols(row, count)], dxr.at[d, :, cols(row, count)],
                dx_sem, (d, j), at(lon, there, lat),
            )
            c.start()
            dx_copies.append(c)

    for j in range(PIECES):
        final = j == PIECES - 1
        for c in x_copies[j]:
            c.wait()
        count = x_starts[j + 1] - x_starts[j]
        if j == 0:
            build_shifts(xs, hc[...], jnp.where(lat == 1, 0, H + 1 - count), count + 1)
        else:
            build_shifts(xs, hc[...], walk(x_starts[j], count) + 1, count)
        row = walk(j * step, step)
        stack = jnp.concatenate(
            [xs[q, :, cols(row + p, step)] for p in range(3) for q in range(3)], axis=0
        )
        preact = jnp.dot(w2[...], stack, preferred_element_type=F32) + bias_col
        upstream = ct_ref[:, cols(row, step)].astype(F32)
        grad = (upstream * gelu_slope(preact)).astype(BF)
        gs[1, :, cols(row + 1, step)] = grad
        gedge[j] = edges(grad, row)
        grad_copies = []
        if j == 0:
            grad_copies.append(
                copy(gs.at[1, :, cols(other * (H - 1) + 1, 1)], gs.at[1, :, to_row], grow_sem, (0,), at(lon, chan, other))
            )
        for side in range(2):
            lon_to = lax.rem(lon + (nlon - 1 if side == 0 else 1), nlon)
            tile = gedge.at[j, pl.ds(side * H, H)]
            grad_copies.append(copy(tile, hg.at[j, 1 - side], gcol_sem, (j, side), at(lon_to, chan, lat)))
            if j == 0:
                grad_copies.append(copy(tile, hgo.at[1 - side], gother_sem, (side,), at(lon_to, chan, other)))
        for c in grad_copies:
            c.start()
        for p in range(3):
            for q in range(3):
                here = pl.ds(q * C, C)
                more = nt(grad, xs[q, :, cols(row + p, step)])
                dwp[p, here, :] = more if j == 0 else dwp[p, here, :] + more
            if final:
                dwsend[p] = dwp[p, far, :].astype(BF)
                c = copy(dwsend.at[p], dwcore.at[p], core_sem, (p,), at(lon, chan, other))
                c.start()
                core_copies.append(c)
        pending.append((grad_copies, row))

    input_grad(0)
    rs_copies = []
    for g in range(3):
        core_copies[g].wait()
        summed = dwp[g, pl.ds(base, half), :] + dwcore[g].astype(F32)
        dwp[g, pl.ds(base, half), :] = summed
        zsend[g] = summed.astype(BF)
        rs_copies.append([])
        for d in range(1, nlon):
            there = lax.rem(lon + d, nlon)
            c = copy(
                zsend.at[g, pl.ds(pl.multiple_of(there * quarter, 16), quarter), :],
                zrecv.at[g, d], rs_sem, (g, d), at(there, chan, lat),
            )
            c.start()
            rs_copies[g].append(c)
    for j in range(1, PIECES):
        input_grad(j)
    bias[spot] = nt(jnp.ones((8, L), BF), gs[1, :, pl.ds(W, L)])
    for d in range(1, ring):
        peer = lax.rem(spot + d, ring)
        c = copy(bias.at[spot], bias.at[spot], bias_sem, (d,), at(peer // nlat, chan, lax.rem(peer, nlat)))
        c.start()
        bias_copies.append(c)
    own_rows = pl.ds(pl.multiple_of(base + lon * quarter, 16), quarter)
    ag_copies, fwd_copies = [], []
    for g in range(3):
        total = dwp[g, own_rows, :]
        for d in range(1, nlon):
            rs_copies[g][d - 1].wait()
            total = total + zrecv[g, d].astype(F32)
        gathered[g, own_rows, :] = total.astype(BF)
        ag_copies.append([])
        for d in range(1, nlon):
            c = copy(
                gathered.at[g, own_rows, :], gathered.at[g, own_rows, :], ag_sem, (g, d),
                at(lax.rem(lon + d, nlon), chan, lat),
            )
            c.start()
            ag_copies[g].append(c)

    def finish_dx(j):
        count = dx_starts[j + 1] - dx_starts[j]
        here = cols(walk(dx_starts[j], count), count)
        acc = dxf[mine, here]
        for d in range(1, nchan):
            dx_copies[j * (nchan - 1) + d - 1].wait()
            acc = acc + dxr[d, :, here].astype(F32)
        dx_ref[:, here] = acc.astype(BF)

    for j in range(PIECES - 1):
        finish_dx(j)
    for g in range(3):
        for d in range(nlon):
            if d > 0:
                ag_copies[g][d - 1].wait()
            source = lax.rem(lon + nlon - d, nlon)
            rows = pl.ds(pl.multiple_of(base + source * quarter, 16), quarter)
            c = copy(gathered.at[g, rows, :], gathered.at[g, rows, :], fwd_sem, (g, d), at(lon, chan, other))
            c.start()
            fwd_copies.append(c)
    finish_dx(PIECES - 1)
    for c in bias_copies:
        c.wait()
    db_ref[...] = jnp.sum(bias[...], axis=0)[:1]
    for c in fwd_copies:
        c.wait()
    dw_ref[...] = gathered[...]


def local(nlon, nchan, nlat, inputs, cotangent, weight, bias_vector):
    C, H, W = inputs.shape
    CA = weight.shape[3]
    L = H * W
    step = nlat * nlon * 16
    R = -(-3 * C // step) * step
    half = R // nlat
    sizes = (nlon, nchan, nlat, C, CA, H, W, R)
    wide = (H + 2) * W
    vmem = pl.BlockSpec(memory_space=pltpu.VMEM)
    dma = pltpu.SemaphoreType.DMA
    dx, dw, db = pl.pallas_call(
        functools.partial(kernel, sizes),
        out_shape=(
            jax.ShapeDtypeStruct((C, L), BF),
            jax.ShapeDtypeStruct((3, R, CA), BF),
            jax.ShapeDtypeStruct((1, C), F32),
        ),
        in_specs=[vmem] * 4,
        out_specs=(vmem,) * 3,
        scratch_shapes=[
            pltpu.VMEM((3, CA, wide), BF),
            pltpu.VMEM((nchan, 4 * H, C), BF),
            pltpu.VMEM((CA, 128), BF),
            pltpu.VMEM((2 * H, C), BF),
            pltpu.VMEM((C, 9 * CA), BF),
            pltpu.VMEM((CA, 9 * C), BF),
            pltpu.VMEM((3, C, wide), BF),
            pltpu.VMEM((PIECES, 2, H, C), BF),
            pltpu.VMEM((2, H, C), BF),
            pltpu.VMEM((PIECES, 2 * H, C), BF),
            pltpu.VMEM((3, R, CA), F32),
            pltpu.VMEM((3, half, CA), BF),
            pltpu.VMEM((3, half, CA), BF),
            pltpu.VMEM((3, half, CA), BF),
            pltpu.VMEM((3, nlon, half // nlon, CA), BF),
            pltpu.VMEM((3, R, CA), BF),
            pltpu.VMEM((nlon * nlat, 8, C), F32),
            pltpu.VMEM((CA, L), F32),
            pltpu.VMEM((CA, L), BF),
            pltpu.VMEM((nchan, C, L), BF),
            dma((2, nchan, PIECES)),
            dma((2, nchan)),
            dma((2, nchan, 2, 2)),
            dma((2, 1)),
            dma((2, PIECES, 2)),
            dma((2, 2)),
            dma((2, 3)),
            dma((2, 3, nlon)),
            dma((2, 3, nlon)),
            dma((2, 3, nlon)),
            dma((2, nlon * nlat)),
            dma((2, nchan, PIECES)),
        ],
        compiler_params=pltpu.CompilerParams(
            collective_id=0, has_side_effects=True, vmem_limit_bytes=48 * 1024 * 1024
        ),
        cost_estimate=pl.CostEstimate(
            flops=3 * 2 * 9 * C * CA * L, bytes_accessed=4 * C * L * 2, transcendentals=2 * C * L
        ),
        name="conv_backward",
    )(
        inputs.reshape(C, L),
        cotangent.reshape(C, L),
        weight.reshape(9 * C, CA),
        bias_vector.reshape(1, C),
    )
    weight_grad = dw[:, : 3 * C].astype(F32).reshape(3, 3, C, CA)
    return dx.reshape(C, H, W), weight_grad, db.reshape(C)


def solution(mesh):
    shape = mesh.shape
    placed = (
        P("chan", ("groups", "lat"), "lon"),
        P("chan", ("groups", "lat"), "lon"),
        P(None, None, "chan", None),
        P("chan"),
    )
    return jax.shard_map(
        functools.partial(local, shape["lon"], shape["chan"], shape["lat"]),
        mesh=mesh,
        in_specs=placed,
        out_specs=(
            P("chan", ("groups", "lat"), "lon"),
            P("groups", None, "chan", None),
            P(("groups", "chan")),
        ),
        check_vma=False,
    )
```

```python
import functools

import jax
import jax.numpy as jnp
from jax import lax
from jax.experimental import pallas as pl
from jax.experimental.pallas import tpu as pltpu
from jax.sharding import PartitionSpec as P

MESH = pl.DeviceIdType.MESH
BF = jnp.bfloat16
F32 = jnp.float32
PIECES = 4


def gelu_slope(preact):
    normal_cdf = 0.5 * (1.0 + lax.erf(preact * 0.7071067811865476))
    density = jnp.exp(-0.5 * preact * preact) * 0.3989422804014327
    return normal_cdf + preact * density


def nt(a, b):
    return lax.dot_general(a, b, (((1,), (1,)), ((), ())), preferred_element_type=F32)


def kernel(
    sizes,
    x_ref, ct_ref, w_ref, b_ref,
    dx_ref, dw_ref, db_ref,
    xs, hx, hc, edge, w2, wt, gs, hg, hgo, gedge,
    dwp, dwsend, dwcore, zsend, zpair, zlast, zrecv, gathered, bias, dxf, dxs, dxr,
    x_sem, row_sem, col_sem, grow_sem, gcol_sem, gother_sem, core_sem, pair_sem, rs_sem, ag_sem, ag_pair_sem, fwd_sem, bias_sem, dx_sem,
):
    nlon, nchan, nlat, C, CA, H, W, R = sizes
    L = H * W
    group = lax.axis_index("groups")
    lon = lax.axis_index("lon")
    chan = lax.axis_index("chan")
    lat = lax.axis_index("lat")
    other = 1 - lat

    def at(a, b, c):
        return (group, a, b, c)

    def copy(src, dst, sems, index, device):
        return pltpu.make_async_remote_copy(
            src_ref=src, dst_ref=dst,
            send_sem=sems.at[(0,) + index], recv_sem=sems.at[(1,) + index],
            device_id=device, device_id_type=MESH,
        )

    everyone = nlon * nchan * nlat
    me = (lon * nchan + chan) * nlat + lat
    barrier = pltpu.get_barrier_semaphore()

    @pl.loop(1, everyone)
    def _(d):
        peer = lax.rem(me + d, everyone)
        pl.semaphore_signal(
            barrier, inc=1, device_id_type=MESH,
            device_id=at(peer // (nchan * nlat), lax.rem(peer // nlat, nchan), lax.rem(peer, nlat)),
        )

    def edges(field, start):
        rows, lanes = 2 * H, field.shape[1]
        row = lax.broadcasted_iota(jnp.int32, (rows, lanes), 0)
        lane = lax.broadcasted_iota(jnp.int32, (rows, lanes), 1) + start * W
        want = jnp.where(row < H, row * W, (row - H) * W + W - 1)
        pick = jnp.where(lane == want, 1.0, 0.0).astype(BF)
        return nt(pick, field).astype(BF)

    def walk(start, count):
        return jnp.where(lat == 1, start, H - start - count)

    def cols(row, count):
        return pl.ds(pl.multiple_of(row * W, W), count * W)

    edge[...] = edges(x_ref[...], 0)
    mine = pl.ds(pl.multiple_of(chan * C, C), C)
    xs[1, mine, pl.ds(W, L)] = x_ref[...]
    rim = cols(lat * (H + 1), 1)
    for q in range(3):
        xs[q, :, rim] = jnp.zeros((CA, W), BF)
        gs[q, :, rim] = jnp.zeros((C, W), BF)
    pl.semaphore_wait(barrier, everyone - 1)

    from_row = cols(other * (H - 1), 1)
    to_row = rim
    halo_copies = []
    for d in range(nchan):
        there = lax.rem(chan + d, nchan)
        halo_copies.append(
            copy(x_ref.at[:, from_row], xs.at[1, mine, to_row], row_sem, (d,), at(lon, there, other))
        )
        for side in range(2):
            lon_to = lax.rem(lon + (nlon - 1 if side == 0 else 1), nlon)
            for dl in range(2):
                halo_copies.append(
                    copy(
                        edge.at[pl.ds(side * H, H)],
                        hx.at[chan, pl.ds(((1 - side) * 2 + dl) * H, H)],
                        col_sem, (d, side, dl),
                        at(lon_to, there, lat if dl == 0 else other),
                    )
                )
    step = H // PIECES
    x_starts = [0] + [step * j + 1 for j in range(1, PIECES)] + [H]
    x_copies = []
    for j in range(PIECES):
        count = x_starts[j + 1] - x_starts[j]
        row = walk(x_starts[j], count)
        x_copies.append([
            copy(
                x_ref.at[:, cols(row, count)], xs.at[1, mine, cols(row + 1, count)],
                x_sem, (d, j), at(lon, lax.rem(chan + d, nchan), lat),
            )
            for d in range(1, nchan)
        ])
        for c in x_copies[j]:
            c.start()
        if j == 0:
            for c in halo_copies:
                c.start()

    for t in range(9):
        w2[:, pl.ds(t * CA, CA)] = w_ref[pl.ds(t * C, C), :]
    wt[...] = jnp.transpose(w_ref[...])
    bias_col = jnp.transpose(jnp.broadcast_to(b_ref[...], (128, C)))[:, :1]

    def build_shifts(field, columns, start, count):
        lane = lax.broadcasted_iota(jnp.int32, columns.shape, 1)
        for i in range(count):
            r = start + i
            here = cols(r, 1)
            held = jnp.where(r == 0, 2 * H - 1, jnp.where(r == H + 1, H, r - 1))
            row = field[1, :, here]
            left = pltpu.roll(columns, lax.rem(W - held, W), 1)
            right = pltpu.roll(columns, lax.rem(2 * W - 1 - 2 * H - held, W), 1)
            field[0, :, here] = jnp.where(lane == 0, left, pltpu.roll(row, 1, 1))
            field[2, :, here] = jnp.where(lane == W - 1, right, pltpu.roll(row, W - 1, 1))

    def turned(blocks):
        have = sum(b.shape[0] for b in blocks)
        full = jnp.concatenate(blocks + [jnp.zeros((128 - have, C), BF)], axis=0)
        return jnp.transpose(full)

    for c in halo_copies:
        c.wait()
    for k in range(nchan):
        hc[pl.ds(k * C, C), :] = turned([hx[k]])

    ring = nlon * nlat
    spot = lon * nlat + lat
    group_rows = 3 * C
    half = R // 2
    quarter = half // nlon
    base = pl.multiple_of(lat * half, half)
    far = pl.ds(pl.multiple_of(other * half, half), half)
    core_copies, bias_copies, dx_copies = [], [], []
    dx_starts = [0] + [step * j - 1 for j in range(1, PIECES)] + [H]
    if R > group_rows:
        for g in range(3):
            dwp[g, pl.ds(group_rows, R - group_rows), :] = jnp.zeros((R - group_rows, CA), F32)
    pending = []

    def input_grad(j):
        grad_copies, row = pending[j]
        for c in grad_copies:
            c.wait()
        if j == 0:
            sides = turned([hg[j, 0], hgo[0], hg[j, 1], hgo[1]])
            build_shifts(gs, sides, jnp.where(lat == 1, 0, H + 1 - step), step + 1)
        else:
            blank = jnp.zeros((H, C), BF)
            sides = turned([hg[j, 0], blank, hg[j, 1], blank])
            build_shifts(gs, sides, row + 1, step)
        count = dx_starts[j + 1] - dx_starts[j]
        row = walk(dx_starts[j], count)
        stack = jnp.concatenate(
            [gs[2 - q, :, cols(row + 2 - p, count)] for p in range(3) for q in range(3)], axis=0
        )
        whole = jnp.dot(wt[...], stack, preferred_element_type=F32)
        dxf[:, cols(row, count)] = whole
        dxs[:, cols(row, count)] = whole.astype(BF)
        for d in range(1, nchan):
            there = lax.rem(chan + d, nchan)
            theirs = pl.ds(pl.multiple_of(there * C, C), C)
            c = copy(
                dxs.at[theirs, cols(row, count)], dxr.at[d, :, cols(row, count)],
                dx_sem, (d, j), at(lon, there, lat),
            )
            c.start()
            dx_copies.append(c)

    for j in range(PIECES):
        final = j == PIECES - 1
        for c in x_copies[j]:
            c.wait()
        count = x_starts[j + 1] - x_starts[j]
        if j == 0:
            build_shifts(xs, hc[...], jnp.where(lat == 1, 0, H + 1 - count), count + 1)
        else:
            build_shifts(xs, hc[...], walk(x_starts[j], count) + 1, count)
        row = walk(j * step, step)
        stack = jnp.concatenate(
            [xs[q, :, cols(row + p, step)] for p in range(3) for q in range(3)], axis=0
        )
        preact = jnp.dot(w2[...], stack, preferred_element_type=F32) + bias_col
        upstream = ct_ref[:, cols(row, step)].astype(F32)
        grad = (upstream * gelu_slope(preact)).astype(BF)
        gs[1, :, cols(row + 1, step)] = grad
        gedge[j] = edges(grad, row)
        grad_copies = []
        if j == 0:
            grad_copies.append(
                copy(gs.at[1, :, cols(other * (H - 1) + 1, 1)], gs.at[1, :, to_row], grow_sem, (0,), at(lon, chan, other))
            )
        for side in range(2):
            lon_to = lax.rem(lon + (nlon - 1 if side == 0 else 1), nlon)
            tile = gedge.at[j, pl.ds(side * H, H)]
            grad_copies.append(copy(tile, hg.at[j, 1 - side], gcol_sem, (j, side), at(lon_to, chan, lat)))
            if j == 0:
                grad_copies.append(copy(tile, hgo.at[1 - side], gother_sem, (side,), at(lon_to, chan, other)))
        for c in grad_copies:
            c.start()
        for p in range(3):
            for q in range(3):
                here = pl.ds(q * C, C)
                more = nt(grad, xs[q, :, cols(row + p, step)])
                dwp[p, here, :] = more if j == 0 else dwp[p, here, :] + more
            if final:
                dwsend[p] = dwp[p, far, :].astype(BF)
                c = copy(dwsend.at[p], dwcore.at[p], core_sem, (p,), at(lon, chan, other))
                c.start()
                core_copies.append(c)
        pending.append((grad_copies, row))

    twos = nlon // 2
    parity = lax.rem(lon, 2)
    mate = at(lon + 1 - 2 * parity, chan, lat)
    zone = twos * quarter
    own_zone = pl.ds(pl.multiple_of(base + parity * zone, 16), zone)
    mate_zone = pl.ds(pl.multiple_of(base + (1 - parity) * zone, 16), zone)
    place = lon // 2
    own_rows = pl.ds(pl.multiple_of(base + parity * zone + place * quarter, 16), quarter)

    def peers(e):
        there = lax.rem(place + e, twos)
        return there, at(there * 2 + parity, chan, lat)

    pair_copies, rs_copies, ag_copies, ag_pair_copies, fwd_copies = [], [], [], [], []
    input_grad(0)
    for g in range(3):
        core_copies[g].wait()
        dwp[g, pl.ds(base, half), :] = dwp[g, pl.ds(base, half), :] + dwcore[g].astype(F32)
        zsend[g] = dwp[g, mate_zone, :].astype(BF)
        c = copy(zsend.at[g], zpair.at[g], pair_sem, (g,), mate)
        c.start()
        pair_copies.append(c)
    input_grad(1)
    for g in range(3):
        pair_copies[g].wait()
        summed = dwp[g, own_zone, :] + zpair[g].astype(F32)
        dwp[g, own_zone, :] = summed
        zlast[g] = summed.astype(BF)
        rs_copies.append([])
        for e in range(1, twos):
            there, device = peers(e)
            c = copy(
                zlast.at[g, pl.ds(pl.multiple_of(there * quarter, 16), quarter), :],
                zrecv.at[g, e], rs_sem, (g, e), device,
            )
            c.start()
            rs_copies[g].append(c)
    input_grad(2)
    for g in range(3):
        total = dwp[g, own_rows, :]
        for e in range(1, twos):
            rs_copies[g][e - 1].wait()
            total = total + zrecv[g, e].astype(F32)
        gathered[g, own_rows, :] = total.astype(BF)
        ag_copies.append([])
        for e in range(1, twos):
            c = copy(
                gathered.at[g, own_rows, :], gathered.at[g, own_rows, :], ag_sem, (g, e), peers(e)[1]
            )
            c.start()
            ag_copies[g].append(c)
    for j in range(3, PIECES):
        input_grad(j)

    def forward(g, k, rows):
        c = copy(gathered.at[g, rows, :], gathered.at[g, rows, :], fwd_sem, (g, k), at(lon, chan, other))
        c.start()
        fwd_copies.append(c)

    for g in range(3):
        for c in ag_copies[g]:
            c.wait()
        c = copy(gathered.at[g, own_zone, :], gathered.at[g, own_zone, :], ag_pair_sem, (g,), mate)
        c.start()
        ag_pair_copies.append(c)
        forward(g, 0, own_zone)
    bias[spot] = nt(jnp.ones((8, L), BF), gs[1, :, pl.ds(W, L)])
    for d in range(1, ring):
        peer = lax.rem(spot + d, ring)
        c = copy(bias.at[spot], bias.at[spot], bias_sem, (d,), at(peer // nlat, chan, lax.rem(peer, nlat)))
        c.start()
        bias_copies.append(c)

    def finish_dx(j):
        count = dx_starts[j + 1] - dx_starts[j]
        here = cols(walk(dx_starts[j], count), count)
        acc = dxf[mine, here]
        for d in range(1, nchan):
            dx_copies[j * (nchan - 1) + d - 1].wait()
            acc = acc + dxr[d, :, here].astype(F32)
        dx_ref[:, here] = acc.astype(BF)

    for j in range(PIECES - 1):
        finish_dx(j)
    for g in range(3):
        ag_pair_copies[g].wait()
        forward(g, 1, mate_zone)
    finish_dx(PIECES - 1)
    for c in bias_copies:
        c.wait()
    db_ref[...] = jnp.sum(bias[...], axis=0)[:1]
    for c in fwd_copies:
        c.wait()
    dw_ref[...] = gathered[...]


def local(nlon, nchan, nlat, inputs, cotangent, weight, bias_vector):
    C, H, W = inputs.shape
    CA = weight.shape[3]
    L = H * W
    step = nlat * nlon * 16
    R = -(-3 * C // step) * step
    half = R // nlat
    sizes = (nlon, nchan, nlat, C, CA, H, W, R)
    wide = (H + 2) * W
    vmem = pl.BlockSpec(memory_space=pltpu.VMEM)
    dma = pltpu.SemaphoreType.DMA
    dx, dw, db = pl.pallas_call(
        functools.partial(kernel, sizes),
        out_shape=(
            jax.ShapeDtypeStruct((C, L), BF),
            jax.ShapeDtypeStruct((3, R, CA), BF),
            jax.ShapeDtypeStruct((1, C), F32),
        ),
        in_specs=[vmem] * 4,
        out_specs=(vmem,) * 3,
        scratch_shapes=[
            pltpu.VMEM((3, CA, wide), BF),
            pltpu.VMEM((nchan, 4 * H, C), BF),
            pltpu.VMEM((CA, 128), BF),
            pltpu.VMEM((2 * H, C), BF),
            pltpu.VMEM((C, 9 * CA), BF),
            pltpu.VMEM((CA, 9 * C), BF),
            pltpu.VMEM((3, C, wide), BF),
            pltpu.VMEM((PIECES, 2, H, C), BF),
            pltpu.VMEM((2, H, C), BF),
            pltpu.VMEM((PIECES, 2 * H, C), BF),
            pltpu.VMEM((3, R, CA), F32),
            pltpu.VMEM((3, half, CA), BF),
            pltpu.VMEM((3, half, CA), BF),
            pltpu.VMEM((3, half // 2, CA), BF),
            pltpu.VMEM((3, half // 2, CA), BF),
            pltpu.VMEM((3, half // 2, CA), BF),
            pltpu.VMEM((3, nlon // 2, half // nlon, CA), BF),
            pltpu.VMEM((3, R, CA), BF),
            pltpu.VMEM((nlon * nlat, 8, C), F32),
            pltpu.VMEM((CA, L), F32),
            pltpu.VMEM((CA, L), BF),
            pltpu.VMEM((nchan, C, L), BF),
            dma((2, nchan, PIECES)),
            dma((2, nchan)),
            dma((2, nchan, 2, 2)),
            dma((2, 1)),
            dma((2, PIECES, 2)),
            dma((2, 2)),
            dma((2, 3)),
            dma((2, 3)),
            dma((2, 3, nlon // 2)),
            dma((2, 3, nlon // 2)),
            dma((2, 3)),
            dma((2, 3, 2)),
            dma((2, nlon * nlat)),
            dma((2, nchan, PIECES)),
        ],
        compiler_params=pltpu.CompilerParams(
            collective_id=0, has_side_effects=True, vmem_limit_bytes=48 * 1024 * 1024
        ),
        cost_estimate=pl.CostEstimate(
            flops=3 * 2 * 9 * C * CA * L, bytes_accessed=4 * C * L * 2, transcendentals=2 * C * L
        ),
        name="conv_backward",
    )(
        inputs.reshape(C, L),
        cotangent.reshape(C, L),
        weight.reshape(9 * C, CA),
        bias_vector.reshape(1, C),
    )
    weight_grad = dw[:, : 3 * C].astype(F32).reshape(3, 3, C, CA)
    return dx.reshape(C, H, W), weight_grad, db.reshape(C)


def solution(mesh):
    shape = mesh.shape
    placed = (
        P("chan", ("groups", "lat"), "lon"),
        P("chan", ("groups", "lat"), "lon"),
        P(None, None, "chan", None),
        P("chan"),
    )
    return jax.shard_map(
        functools.partial(local, shape["lon"], shape["chan"], shape["lat"]),
        mesh=mesh,
        in_specs=placed,
        out_specs=(
            P("chan", ("groups", "lat"), "lon"),
            P("groups", None, "chan", None),
            P(("groups", "chan")),
        ),
        check_vma=False,
    )
```

```python
import functools

import jax
import jax.numpy as jnp
from jax import lax
from jax.experimental import pallas as pl
from jax.experimental.pallas import tpu as pltpu
from jax.sharding import PartitionSpec as P

MESH = pl.DeviceIdType.MESH
BF = jnp.bfloat16
F32 = jnp.float32
PIECES = 4


def gelu_slope(preact):
    normal_cdf = 0.5 * (1.0 + lax.erf(preact * 0.7071067811865476))
    density = jnp.exp(-0.5 * preact * preact) * 0.3989422804014327
    return normal_cdf + preact * density


def nt(a, b):
    return lax.dot_general(a, b, (((1,), (1,)), ((), ())), preferred_element_type=F32)


def kernel(
    sizes,
    x_ref, ct_ref, w_ref, b_ref,
    dx_ref, dw_ref, db_ref,
    xs, hx, hc, edge, w2, wt, gs, hg, hgo, gedge,
    dwp, dwsend, dwcore, zsend, zrecv, gathered, bias, dxf, dxs, dxr,
    x_sem, row_sem, col_sem, grow_sem, gcol_sem, gother_sem, core_sem, rs_sem, ag_sem, fwd_sem, bias_sem, dx_sem,
):
    nlon, nchan, nlat, C, CA, H, W, R = sizes
    L = H * W
    group = lax.axis_index("groups")
    lon = lax.axis_index("lon")
    chan = lax.axis_index("chan")
    lat = lax.axis_index("lat")
    other = 1 - lat

    def at(a, b, c):
        return (group, a, b, c)

    def copy(src, dst, sems, index, device):
        return pltpu.make_async_remote_copy(
            src_ref=src, dst_ref=dst,
            send_sem=sems.at[(0,) + index], recv_sem=sems.at[(1,) + index],
            device_id=device, device_id_type=MESH,
        )

    everyone = nlon * nchan * nlat
    me = (lon * nchan + chan) * nlat + lat
    barrier = pltpu.get_barrier_semaphore()

    @pl.loop(1, everyone)
    def _(d):
        peer = lax.rem(me + d, everyone)
        pl.semaphore_signal(
            barrier, inc=1, device_id_type=MESH,
            device_id=at(peer // (nchan * nlat), lax.rem(peer // nlat, nchan), lax.rem(peer, nlat)),
        )

    def edges(field, start):
        rows, lanes = 2 * H, field.shape[1]
        row = lax.broadcasted_iota(jnp.int32, (rows, lanes), 0)
        lane = lax.broadcasted_iota(jnp.int32, (rows, lanes), 1) + start * W
        want = jnp.where(row < H, row * W, (row - H) * W + W - 1)
        pick = jnp.where(lane == want, 1.0, 0.0).astype(BF)
        return nt(pick, field).astype(BF)

    def walk(start, count):
        return jnp.where(lat == 1, start, H - start - count)

    def cols(row, count):
        return pl.ds(pl.multiple_of(row * W, W), count * W)

    edge[...] = edges(x_ref[...], 0)
    mine = pl.ds(pl.multiple_of(chan * C, C), C)
    xs[1, mine, pl.ds(W, L)] = x_ref[...]
    rim = cols(lat * (H + 1), 1)
    for q in range(3):
        xs[q, :, rim] = jnp.zeros((CA, W), BF)
        gs[q, :, rim] = jnp.zeros((C, W), BF)
    pl.semaphore_wait(barrier, everyone - 1)

    from_row = cols(other * (H - 1), 1)
    to_row = rim
    halo_copies = []
    for d in range(nchan):
        there = lax.rem(chan + d, nchan)
        halo_copies.append(
            copy(x_ref.at[:, from_row], xs.at[1, mine, to_row], row_sem, (d,), at(lon, there, other))
        )
        for side in range(2):
            lon_to = lax.rem(lon + (nlon - 1 if side == 0 else 1), nlon)
            for dl in range(2):
                halo_copies.append(
                    copy(
                        edge.at[pl.ds(side * H, H)],
                        hx.at[chan, pl.ds(((1 - side) * 2 + dl) * H, H)],
                        col_sem, (d, side, dl),
                        at(lon_to, there, lat if dl == 0 else other),
                    )
                )
    for c in halo_copies:
        c.start()
    g_starts = [H * k // 16 for k in (0, 4, 8, 12, 16)]
    x_starts = [0] + [k + 1 for k in g_starts[1:-1]] + [H]
    x_copies = []
    for j in range(PIECES):
        count = x_starts[j + 1] - x_starts[j]
        row = walk(x_starts[j], count)
        x_copies.append([
            copy(
                x_ref.at[:, cols(row, count)], xs.at[1, mine, cols(row + 1, count)],
                x_sem, (d, j), at(lon, lax.rem(chan + d, nchan), lat),
            )
            for d in range(1, nchan)
        ])
        for c in x_copies[j]:
            c.start()

    for t in range(9):
        w2[:, pl.ds(t * CA, CA)] = w_ref[pl.ds(t * C, C), :]
    wt[...] = jnp.transpose(w_ref[...])
    bias_col = jnp.transpose(jnp.broadcast_to(b_ref[...], (128, C)))[:, :1]

    def build_shifts(field, who, columns, start, count):
        lane = lax.broadcasted_iota(jnp.int32, columns.shape, 1)
        for i in range(count):
            r = start + i
            here = cols(r, 1)
            held = jnp.where(r == 0, 2 * H - 1, jnp.where(r == H + 1, H, r - 1))
            row = field[1, who, here]
            left = pltpu.roll(columns, lax.rem(W - held, W), 1)
            right = pltpu.roll(columns, lax.rem(2 * W - 1 - 2 * H - held, W), 1)
            field[0, who, here] = jnp.where(lane == 0, left, pltpu.roll(row, 1, 1))
            field[2, who, here] = jnp.where(lane == W - 1, right, pltpu.roll(row, W - 1, 1))

    def turned(blocks):
        have = sum(b.shape[0] for b in blocks)
        full = jnp.concatenate(blocks + [jnp.zeros((128 - have, C), BF)], axis=0)
        return jnp.transpose(full)

    def channels(d):
        return pl.ds(pl.multiple_of(lax.rem(chan + d, nchan) * C, C), C)

    def shift_inputs(d, j):
        who = channels(d)
        count = x_starts[j + 1] - x_starts[j]
        if j == 0:
            build_shifts(xs, who, hc[who, :], jnp.where(lat == 1, 0, H + 1 - count), count + 1)
        else:
            build_shifts(xs, who, hc[who, :], walk(x_starts[j], count) + 1, count)

    for d in range(nchan):
        back = lax.rem(chan + nchan - d, nchan)
        for c in halo_copies[d * 5 : d * 5 + 5]:
            c.wait()
        hc[pl.ds(pl.multiple_of(back * C, C), C), :] = turned([hx[back]])
        if d == 0:
            for j in range(PIECES):
                shift_inputs(0, j)

    ring = nlon * nlat
    spot = lon * nlat + lat
    group_rows = 3 * C
    half = R // 2
    quarter = half // nlon
    base = pl.multiple_of(lat * half, half)
    far = pl.ds(pl.multiple_of(other * half, half), half)
    core_copies, bias_copies, dx_copies = [], [], []
    dx_starts = [0] + [k - 1 for k in g_starts[1:-1]] + [H]
    if R > group_rows:
        for g in range(3):
            dwp[g, pl.ds(group_rows, R - group_rows), :] = jnp.zeros((R - group_rows, CA), F32)
    pending = []

    def input_grad(j):
        grad_copies, row = pending[j]
        step = g_starts[j + 1] - g_starts[j]
        for c in grad_copies:
            c.wait()
        if j == 0:
            sides = turned([hg[j, 0], hgo[0], hg[j, 1], hgo[1]])
            build_shifts(gs, slice(None), sides, jnp.where(lat == 1, 0, H + 1 - step), step + 1)
        else:
            blank = jnp.zeros((H, C), BF)
            sides = turned([hg[j, 0], blank, hg[j, 1], blank])
            build_shifts(gs, slice(None), sides, row + 1, step)
        count = dx_starts[j + 1] - dx_starts[j]
        row = walk(dx_starts[j], count)
        stack = jnp.concatenate(
            [gs[2 - q, :, cols(row + 2 - p, count)] for p in range(3) for q in range(3)], axis=0
        )
        whole = jnp.dot(wt[...], stack, preferred_element_type=F32)
        dxf[:, cols(row, count)] = whole
        dxs[:, cols(row, count)] = whole.astype(BF)
        for d in range(1, nchan):
            there = lax.rem(chan + d, nchan)
            theirs = pl.ds(pl.multiple_of(there * C, C), C)
            c = copy(
                dxs.at[theirs, cols(row, count)], dxr.at[d, :, cols(row, count)],
                dx_sem, (d, j), at(lon, there, lat),
            )
            c.start()
            dx_copies.append(c)

    for j in range(PIECES):
        final = j == PIECES - 1
        for c in x_copies[j]:
            c.wait()
        for d in range(1, nchan):
            shift_inputs(d, j)
        step = g_starts[j + 1] - g_starts[j]
        row = walk(g_starts[j], step)
        stack = jnp.concatenate(
            [xs[q, :, cols(row + p, step)] for p in range(3) for q in range(3)], axis=0
        )
        preact = jnp.dot(w2[...], stack, preferred_element_type=F32) + bias_col
        upstream = ct_ref[:, cols(row, step)].astype(F32)
        grad = (upstream * gelu_slope(preact)).astype(BF)
        gs[1, :, cols(row + 1, step)] = grad
        gedge[j] = edges(grad, row)
        grad_copies = []
        if j == 0:
            grad_copies.append(
                copy(gs.at[1, :, cols(other * (H - 1) + 1, 1)], gs.at[1, :, to_row], grow_sem, (0,), at(lon, chan, other))
            )
        for side in range(2):
            lon_to = lax.rem(lon + (nlon - 1 if side == 0 else 1), nlon)
            tile = gedge.at[j, pl.ds(side * H, H)]
            grad_copies.append(copy(tile, hg.at[j, 1 - side], gcol_sem, (j, side), at(lon_to, chan, lat)))
            if j == 0:
                grad_copies.append(copy(tile, hgo.at[1 - side], gother_sem, (side,), at(lon_to, chan, other)))
        for c in grad_copies:
            c.start()
        for p in range(3):
            for q in range(3):
                here = pl.ds(q * C, C)
                more = nt(grad, xs[q, :, cols(row + p, step)])
                dwp[p, here, :] = more if j == 0 else dwp[p, here, :] + more
            if final:
                dwsend[p] = dwp[p, far, :].astype(BF)
                c = copy(dwsend.at[p], dwcore.at[p], core_sem, (p,), at(lon, chan, other))
                c.start()
                core_copies.append(c)
        pending.append((grad_copies, row))

    input_grad(0)
    rs_copies = []
    for g in range(3):
        core_copies[g].wait()
        summed = dwp[g, pl.ds(base, half), :] + dwcore[g].astype(F32)
        dwp[g, pl.ds(base, half), :] = summed
        zsend[g] = summed.astype(BF)
        rs_copies.append([])
        for d in range(1, nlon):
            there = lax.rem(lon + d, nlon)
            c = copy(
                zsend.at[g, pl.ds(pl.multiple_of(there * quarter, 16), quarter), :],
                zrecv.at[g, d], rs_sem, (g, d), at(there, chan, lat),
            )
            c.start()
            rs_copies[g].append(c)
    for j in range(1, PIECES):
        input_grad(j)
    bias[spot] = nt(jnp.ones((8, L), BF), gs[1, :, pl.ds(W, L)])
    for d in range(1, ring):
        peer = lax.rem(spot + d, ring)
        c = copy(bias.at[spot], bias.at[spot], bias_sem, (d,), at(peer // nlat, chan, lax.rem(peer, nlat)))
        c.start()
        bias_copies.append(c)
    own_rows = pl.ds(pl.multiple_of(base + lon * quarter, 16), quarter)
    ag_copies, fwd_copies = [], []
    for g in range(3):
        total = dwp[g, own_rows, :]
        for d in range(1, nlon):
            rs_copies[g][d - 1].wait()
            total = total + zrecv[g, d].astype(F32)
        gathered[g, own_rows, :] = total.astype(BF)
        ag_copies.append([])
        for d in range(1, nlon):
            c = copy(
                gathered.at[g, own_rows, :], gathered.at[g, own_rows, :], ag_sem, (g, d),
                at(lax.rem(lon + d, nlon), chan, lat),
            )
            c.start()
            ag_copies[g].append(c)

    def finish_dx(j):
        count = dx_starts[j + 1] - dx_starts[j]
        here = cols(walk(dx_starts[j], count), count)
        acc = dxf[mine, here]
        for d in range(1, nchan):
            dx_copies[j * (nchan - 1) + d - 1].wait()
            acc = acc + dxr[d, :, here].astype(F32)
        dx_ref[:, here] = acc.astype(BF)

    for j in range(PIECES - 1):
        finish_dx(j)
    for g in range(3):
        for d in range(nlon):
            if d > 0:
                ag_copies[g][d - 1].wait()
            source = lax.rem(lon + nlon - d, nlon)
            rows = pl.ds(pl.multiple_of(base + source * quarter, 16), quarter)
            c = copy(gathered.at[g, rows, :], gathered.at[g, rows, :], fwd_sem, (g, d), at(lon, chan, other))
            c.start()
            fwd_copies.append(c)
    finish_dx(PIECES - 1)
    for c in bias_copies:
        c.wait()
    db_ref[...] = jnp.sum(bias[...], axis=0)[:1]
    for c in fwd_copies:
        c.wait()
    dw_ref[...] = gathered[...]


def local(nlon, nchan, nlat, inputs, cotangent, weight, bias_vector):
    C, H, W = inputs.shape
    CA = weight.shape[3]
    L = H * W
    step = nlat * nlon * 16
    R = -(-3 * C // step) * step
    half = R // nlat
    sizes = (nlon, nchan, nlat, C, CA, H, W, R)
    wide = (H + 2) * W
    vmem = pl.BlockSpec(memory_space=pltpu.VMEM)
    dma = pltpu.SemaphoreType.DMA
    dx, dw, db = pl.pallas_call(
        functools.partial(kernel, sizes),
        out_shape=(
            jax.ShapeDtypeStruct((C, L), BF),
            jax.ShapeDtypeStruct((3, R, CA), BF),
            jax.ShapeDtypeStruct((1, C), F32),
        ),
        in_specs=[vmem] * 4,
        out_specs=(vmem,) * 3,
        scratch_shapes=[
            pltpu.VMEM((3, CA, wide), BF),
            pltpu.VMEM((nchan, 4 * H, C), BF),
            pltpu.VMEM((CA, 128), BF),
            pltpu.VMEM((2 * H, C), BF),
            pltpu.VMEM((C, 9 * CA), BF),
            pltpu.VMEM((CA, 9 * C), BF),
            pltpu.VMEM((3, C, wide), BF),
            pltpu.VMEM((PIECES, 2, H, C), BF),
            pltpu.VMEM((2, H, C), BF),
            pltpu.VMEM((PIECES, 2 * H, C), BF),
            pltpu.VMEM((3, R, CA), F32),
            pltpu.VMEM((3, half, CA), BF),
            pltpu.VMEM((3, half, CA), BF),
            pltpu.VMEM((3, half, CA), BF),
            pltpu.VMEM((3, nlon, half // nlon, CA), BF),
            pltpu.VMEM((3, R, CA), BF),
            pltpu.VMEM((nlon * nlat, 8, C), F32),
            pltpu.VMEM((CA, L), F32),
            pltpu.VMEM((CA, L), BF),
            pltpu.VMEM((nchan, C, L), BF),
            dma((2, nchan, PIECES)),
            dma((2, nchan)),
            dma((2, nchan, 2, 2)),
            dma((2, 1)),
            dma((2, PIECES, 2)),
            dma((2, 2)),
            dma((2, 3)),
            dma((2, 3, nlon)),
            dma((2, 3, nlon)),
            dma((2, 3, nlon)),
            dma((2, nlon * nlat)),
            dma((2, nchan, PIECES)),
        ],
        compiler_params=pltpu.CompilerParams(
            collective_id=0, has_side_effects=True, vmem_limit_bytes=48 * 1024 * 1024
        ),
        cost_estimate=pl.CostEstimate(
            flops=3 * 2 * 9 * C * CA * L, bytes_accessed=4 * C * L * 2, transcendentals=2 * C * L
        ),
        name="conv_backward",
    )(
        inputs.reshape(C, L),
        cotangent.reshape(C, L),
        weight.reshape(9 * C, CA),
        bias_vector.reshape(1, C),
    )
    weight_grad = dw[:, : 3 * C].astype(F32).reshape(3, 3, C, CA)
    return dx.reshape(C, H, W), weight_grad, db.reshape(C)


def solution(mesh):
    shape = mesh.shape
    placed = (
        P("chan", ("groups", "lat"), "lon"),
        P("chan", ("groups", "lat"), "lon"),
        P(None, None, "chan", None),
        P("chan"),
    )
    return jax.shard_map(
        functools.partial(local, shape["lon"], shape["chan"], shape["lat"]),
        mesh=mesh,
        in_specs=placed,
        out_specs=(
            P("chan", ("groups", "lat"), "lon"),
            P("groups", None, "chan", None),
            P(("groups", "chan")),
        ),
        check_vma=False,
    )
```

```python
import functools

import jax
import jax.numpy as jnp
from jax import lax
from jax.experimental import pallas as pl
from jax.experimental.pallas import tpu as pltpu
from jax.sharding import PartitionSpec as P

MESH = pl.DeviceIdType.MESH
BF = jnp.bfloat16
F32 = jnp.float32
PIECES = 4


def gelu_slope(preact):
    normal_cdf = 0.5 * (1.0 + lax.erf(preact * 0.7071067811865476))
    density = jnp.exp(-0.5 * preact * preact) * 0.3989422804014327
    return normal_cdf + preact * density


def nt(a, b):
    return lax.dot_general(a, b, (((1,), (1,)), ((), ())), preferred_element_type=F32)


def kernel(
    sizes,
    x_ref, ct_ref, w_ref, b_ref,
    dx_ref, dw_ref, db_ref,
    xs, hx, hc, edge, w2, wt, gs, hg, hgo, gedge,
    dwp, dwsend, dwcore, zsend, zrecv, gathered, bias, dxf, dxs, dxr,
    x_sem, row_sem, col_sem, grow_sem, gcol_sem, gother_sem, core_sem, rs_sem, ag_sem, fwd_sem, bias_sem, dx_sem,
):
    nlon, nchan, nlat, C, CA, H, W, R = sizes
    L = H * W
    group = lax.axis_index("groups")
    lon = lax.axis_index("lon")
    chan = lax.axis_index("chan")
    lat = lax.axis_index("lat")
    other = 1 - lat

    def at(a, b, c):
        return (group, a, b, c)

    def copy(src, dst, sems, index, device):
        return pltpu.make_async_remote_copy(
            src_ref=src, dst_ref=dst,
            send_sem=sems.at[(0,) + index], recv_sem=sems.at[(1,) + index],
            device_id=device, device_id_type=MESH,
        )

    everyone = nlon * nchan * nlat
    me = (lon * nchan + chan) * nlat + lat
    barrier = pltpu.get_barrier_semaphore()

    @pl.loop(1, everyone)
    def _(d):
        peer = lax.rem(me + d, everyone)
        pl.semaphore_signal(
            barrier, inc=1, device_id_type=MESH,
            device_id=at(peer // (nchan * nlat), lax.rem(peer // nlat, nchan), lax.rem(peer, nlat)),
        )

    def edges(field, start):
        rows, lanes = 2 * H, field.shape[1]
        row = lax.broadcasted_iota(jnp.int32, (rows, lanes), 0)
        lane = lax.broadcasted_iota(jnp.int32, (rows, lanes), 1) + start * W
        want = jnp.where(row < H, row * W, (row - H) * W + W - 1)
        pick = jnp.where(lane == want, 1.0, 0.0).astype(BF)
        return nt(pick, field).astype(BF)

    def walk(start, count):
        return jnp.where(lat == 1, start, H - start - count)

    def cols(row, count):
        return pl.ds(pl.multiple_of(row * W, W), count * W)

    edge[...] = edges(x_ref[...], 0)
    mine = pl.ds(pl.multiple_of(chan * C, C), C)
    xs[1, mine, pl.ds(W, L)] = x_ref[...]
    rim = cols(lat * (H + 1), 1)
    for q in range(3):
        xs[q, :, rim] = jnp.zeros((CA, W), BF)
        gs[q, :, rim] = jnp.zeros((C, W), BF)
    pl.semaphore_wait(barrier, everyone - 1)

    from_row = cols(other * (H - 1), 1)
    to_row = rim
    halo_copies = []
    for d in range(nchan):
        there = lax.rem(chan + d, nchan)
        halo_copies.append(
            copy(x_ref.at[:, from_row], xs.at[1, mine, to_row], row_sem, (d,), at(lon, there, other))
        )
        for side in range(2):
            lon_to = lax.rem(lon + (nlon - 1 if side == 0 else 1), nlon)
            for dl in range(2):
                halo_copies.append(
                    copy(
                        edge.at[pl.ds(side * H, H)],
                        hx.at[chan, pl.ds(((1 - side) * 2 + dl) * H, H)],
                        col_sem, (d, side, dl),
                        at(lon_to, there, lat if dl == 0 else other),
                    )
                )
    for c in halo_copies:
        c.start()
    step = H // PIECES
    x_starts = [0] + [step * j + 1 for j in range(1, PIECES)] + [H]
    x_copies = []
    for j in range(PIECES):
        count = x_starts[j + 1] - x_starts[j]
        row = walk(x_starts[j], count)
        x_copies.append([
            copy(
                x_ref.at[:, cols(row, count)], xs.at[1, mine, cols(row + 1, count)],
                x_sem, (d, j), at(lon, lax.rem(chan + d, nchan), lat),
            )
            for d in range(1, nchan)
        ])
        for c in x_copies[j]:
            c.start()

    for t in range(9):
        w2[:, pl.ds(t * CA, CA)] = w_ref[pl.ds(t * C, C), :]
    bias_col = jnp.transpose(jnp.broadcast_to(b_ref[...], (128, C)))[:, :1]

    def build_shifts(field, columns, start, count):
        lane = lax.broadcasted_iota(jnp.int32, columns.shape, 1)
        for i in range(count):
            r = start + i
            here = cols(r, 1)
            held = jnp.where(r == 0, 2 * H - 1, jnp.where(r == H + 1, H, r - 1))
            row = field[1, :, here]
            left = pltpu.roll(columns, lax.rem(W - held, W), 1)
            right = pltpu.roll(columns, lax.rem(2 * W - 1 - 2 * H - held, W), 1)
            field[0, :, here] = jnp.where(lane == 0, left, pltpu.roll(row, 1, 1))
            field[2, :, here] = jnp.where(lane == W - 1, right, pltpu.roll(row, W - 1, 1))

    def turned(blocks):
        have = sum(b.shape[0] for b in blocks)
        full = jnp.concatenate(blocks + [jnp.zeros((128 - have, C), BF)], axis=0)
        return jnp.transpose(full)

    for c in halo_copies:
        c.wait()
    for k in range(nchan):
        hc[pl.ds(k * C, C), :] = turned([hx[k]])

    ring = nlon * nlat
    spot = lon * nlat + lat
    group_rows = 3 * C
    half = R // 2
    quarter = half // nlon
    base = pl.multiple_of(lat * half, half)
    far = pl.ds(pl.multiple_of(other * half, half), half)
    core_copies, bias_copies, dx_copies = [], [], []
    dx_starts = [0] + [step * j - 1 for j in range(1, PIECES)] + [H]
    if R > group_rows:
        for g in range(3):
            dwp[g, pl.ds(group_rows, R - group_rows), :] = jnp.zeros((R - group_rows, CA), F32)
    grad_copies = []

    def input_grad(j):
        if j == 0:
            for c in grad_copies:
                c.wait()
            sides = turned([hg[0], hgo[0], hg[1], hgo[1]])
            build_shifts(gs, sides, other, H + 1)
        count = dx_starts[j + 1] - dx_starts[j]
        row = walk(dx_starts[j], count)
        stack = jnp.concatenate(
            [gs[2 - q, :, cols(row + 2 - p, count)] for p in range(3) for q in range(3)], axis=0
        )
        whole = jnp.dot(wt[...], stack, preferred_element_type=F32)
        dxf[:, cols(row, count)] = whole
        dxs[:, cols(row, count)] = whole.astype(BF)
        for d in range(1, nchan):
            there = lax.rem(chan + d, nchan)
            theirs = pl.ds(pl.multiple_of(there * C, C), C)
            c = copy(
                dxs.at[theirs, cols(row, count)], dxr.at[d, :, cols(row, count)],
                dx_sem, (d, j), at(lon, there, lat),
            )
            c.start()
            dx_copies.append(c)

    for j in range(PIECES):
        final = j == PIECES - 1
        for c in x_copies[j]:
            c.wait()
        count = x_starts[j + 1] - x_starts[j]
        if j == 0:
            build_shifts(xs, hc[...], jnp.where(lat == 1, 0, H + 1 - count), count + 1)
        else:
            build_shifts(xs, hc[...], walk(x_starts[j], count) + 1, count)
        row = walk(j * step, step)
        stack = jnp.concatenate(
            [xs[q, :, cols(row + p, step)] for p in range(3) for q in range(3)], axis=0
        )
        preact = jnp.dot(w2[...], stack, preferred_element_type=F32) + bias_col
        upstream = ct_ref[:, cols(row, step)].astype(F32)
        grad = (upstream * gelu_slope(preact)).astype(BF)
        gs[1, :, cols(row + 1, step)] = grad
        if final:
            gedge[...] = edges(gs[1, :, pl.ds(W, L)], 0)
            grad_copies.append(
                copy(gs.at[1, :, cols(other * (H - 1) + 1, 1)], gs.at[1, :, to_row], grow_sem, (0,), at(lon, chan, other))
            )
            for side in range(2):
                lon_to = lax.rem(lon + (nlon - 1 if side == 0 else 1), nlon)
                tile = gedge.at[pl.ds(side * H, H)]
                grad_copies.append(copy(tile, hg.at[1 - side], gcol_sem, (side,), at(lon_to, chan, lat)))
                grad_copies.append(copy(tile, hgo.at[1 - side], gother_sem, (side,), at(lon_to, chan, other)))
            for c in grad_copies:
                c.start()
        for p in range(3):
            for q in range(3):
                here = pl.ds(q * C, C)
                more = nt(grad, xs[q, :, cols(row + p, step)])
                dwp[p, here, :] = more if j == 0 else dwp[p, here, :] + more
            if final:
                dwsend[p] = dwp[p, far, :].astype(BF)
                c = copy(dwsend.at[p], dwcore.at[p], core_sem, (p,), at(lon, chan, other))
                c.start()
                core_copies.append(c)

    wt[...] = jnp.transpose(w_ref[...])
    rs_copies = []
    for g in range(3):
        core_copies[g].wait()
        summed = dwp[g, pl.ds(base, half), :] + dwcore[g].astype(F32)
        dwp[g, pl.ds(base, half), :] = summed
        zsend[g] = summed.astype(BF)
        rs_copies.append([])
        for d in range(1, nlon):
            there = lax.rem(lon + d, nlon)
            c = copy(
                zsend.at[g, pl.ds(pl.multiple_of(there * quarter, 16), quarter), :],
                zrecv.at[g, d], rs_sem, (g, d), at(there, chan, lat),
            )
            c.start()
            rs_copies[g].append(c)
    for j in range(PIECES):
        input_grad(j)
    bias[spot] = nt(jnp.ones((8, L), BF), gs[1, :, pl.ds(W, L)])
    for d in range(1, ring):
        peer = lax.rem(spot + d, ring)
        c = copy(bias.at[spot], bias.at[spot], bias_sem, (d,), at(peer // nlat, chan, lax.rem(peer, nlat)))
        c.start()
        bias_copies.append(c)
    own_rows = pl.ds(pl.multiple_of(base + lon * quarter, 16), quarter)
    ag_copies, fwd_copies = [], []
    for g in range(3):
        total = dwp[g, own_rows, :]
        for d in range(1, nlon):
            rs_copies[g][d - 1].wait()
            total = total + zrecv[g, d].astype(F32)
        gathered[g, own_rows, :] = total.astype(BF)
        ag_copies.append([])
        for d in range(1, nlon):
            c = copy(
                gathered.at[g, own_rows, :], gathered.at[g, own_rows, :], ag_sem, (g, d),
                at(lax.rem(lon + d, nlon), chan, lat),
            )
            c.start()
            ag_copies[g].append(c)

    def finish_dx(j):
        count = dx_starts[j + 1] - dx_starts[j]
        here = cols(walk(dx_starts[j], count), count)
        acc = dxf[mine, here]
        for d in range(1, nchan):
            dx_copies[j * (nchan - 1) + d - 1].wait()
            acc = acc + dxr[d, :, here].astype(F32)
        dx_ref[:, here] = acc.astype(BF)

    for j in range(PIECES - 1):
        finish_dx(j)
    for g in range(3):
        for d in range(nlon):
            if d > 0:
                ag_copies[g][d - 1].wait()
            source = lax.rem(lon + nlon - d, nlon)
            rows = pl.ds(pl.multiple_of(base + source * quarter, 16), quarter)
            c = copy(gathered.at[g, rows, :], gathered.at[g, rows, :], fwd_sem, (g, d), at(lon, chan, other))
            c.start()
            fwd_copies.append(c)
    finish_dx(PIECES - 1)
    for c in bias_copies:
        c.wait()
    db_ref[...] = jnp.sum(bias[...], axis=0)[:1]
    for c in fwd_copies:
        c.wait()
    dw_ref[...] = gathered[...]


def local(nlon, nchan, nlat, inputs, cotangent, weight, bias_vector):
    C, H, W = inputs.shape
    CA = weight.shape[3]
    L = H * W
    step = nlat * nlon * 16
    R = -(-3 * C // step) * step
    half = R // nlat
    sizes = (nlon, nchan, nlat, C, CA, H, W, R)
    wide = (H + 2) * W
    vmem = pl.BlockSpec(memory_space=pltpu.VMEM)
    dma = pltpu.SemaphoreType.DMA
    dx, dw, db = pl.pallas_call(
        functools.partial(kernel, sizes),
        out_shape=(
            jax.ShapeDtypeStruct((C, L), BF),
            jax.ShapeDtypeStruct((3, R, CA), BF),
            jax.ShapeDtypeStruct((1, C), F32),
        ),
        in_specs=[vmem] * 4,
        out_specs=(vmem,) * 3,
        scratch_shapes=[
            pltpu.VMEM((3, CA, wide), BF),
            pltpu.VMEM((nchan, 4 * H, C), BF),
            pltpu.VMEM((CA, 128), BF),
            pltpu.VMEM((2 * H, C), BF),
            pltpu.VMEM((C, 9 * CA), BF),
            pltpu.VMEM((CA, 9 * C), BF),
            pltpu.VMEM((3, C, wide), BF),
            pltpu.VMEM((2, H, C), BF),
            pltpu.VMEM((2, H, C), BF),
            pltpu.VMEM((2 * H, C), BF),
            pltpu.VMEM((3, R, CA), F32),
            pltpu.VMEM((3, half, CA), BF),
            pltpu.VMEM((3, half, CA), BF),
            pltpu.VMEM((3, half, CA), BF),
            pltpu.VMEM((3, nlon, half // nlon, CA), BF),
            pltpu.VMEM((3, R, CA), BF),
            pltpu.VMEM((nlon * nlat, 8, C), F32),
            pltpu.VMEM((CA, L), F32),
            pltpu.VMEM((CA, L), BF),
            pltpu.VMEM((nchan, C, L), BF),
            dma((2, nchan, PIECES)),
            dma((2, nchan)),
            dma((2, nchan, 2, 2)),
            dma((2, 1)),
            dma((2, 2)),
            dma((2, 2)),
            dma((2, 3)),
            dma((2, 3, nlon)),
            dma((2, 3, nlon)),
            dma((2, 3, nlon)),
            dma((2, nlon * nlat)),
            dma((2, nchan, PIECES)),
        ],
        compiler_params=pltpu.CompilerParams(
            collective_id=0, has_side_effects=True, vmem_limit_bytes=48 * 1024 * 1024
        ),
        cost_estimate=pl.CostEstimate(
            flops=3 * 2 * 9 * C * CA * L, bytes_accessed=4 * C * L * 2, transcendentals=2 * C * L
        ),
        name="conv_backward",
    )(
        inputs.reshape(C, L),
        cotangent.reshape(C, L),
        weight.reshape(9 * C, CA),
        bias_vector.reshape(1, C),
    )
    weight_grad = dw[:, : 3 * C].astype(F32).reshape(3, 3, C, CA)
    return dx.reshape(C, H, W), weight_grad, db.reshape(C)


def solution(mesh):
    shape = mesh.shape
    placed = (
        P("chan", ("groups", "lat"), "lon"),
        P("chan", ("groups", "lat"), "lon"),
        P(None, None, "chan", None),
        P("chan"),
    )
    return jax.shard_map(
        functools.partial(local, shape["lon"], shape["chan"], shape["lat"]),
        mesh=mesh,
        in_specs=placed,
        out_specs=(
            P("chan", ("groups", "lat"), "lon"),
            P("groups", None, "chan", None),
            P(("groups", "chan")),
        ),
        check_vma=False,
    )
```

```python
import functools

import jax
import jax.numpy as jnp
from jax import lax
from jax.experimental import pallas as pl
from jax.experimental.pallas import tpu as pltpu
from jax.sharding import PartitionSpec as P

MESH = pl.DeviceIdType.MESH
BF = jnp.bfloat16
F32 = jnp.float32
PIECES = 4


def gelu_slope(preact):
    normal_cdf = 0.5 * (1.0 + lax.erf(preact * 0.7071067811865476))
    density = jnp.exp(-0.5 * preact * preact) * 0.3989422804014327
    return normal_cdf + preact * density


def nt(a, b):
    return lax.dot_general(a, b, (((1,), (1,)), ((), ())), preferred_element_type=F32)


def kernel(
    sizes,
    x_ref, ct_ref, w_ref, b_ref,
    dx_ref, dw_ref, db_ref,
    xs, hx, hc, edge, w2, wt, gs, hg, hgo, gedge,
    dwp, dwsend, dwcore, zsend, zrecv, gathered, bias, dxf, dxs, dxr,
    x_sem, row_sem, col_sem, grow_sem, gcol_sem, gother_sem, core_sem, rs_sem, ag_sem, fwd_sem, bias_sem, dx_sem,
):
    nlon, nchan, nlat, C, CA, H, W, R = sizes
    L = H * W
    group = lax.axis_index("groups")
    lon = lax.axis_index("lon")
    chan = lax.axis_index("chan")
    lat = lax.axis_index("lat")
    other = 1 - lat

    def at(a, b, c):
        return (group, a, b, c)

    def copy(src, dst, sems, index, device):
        return pltpu.make_async_remote_copy(
            src_ref=src, dst_ref=dst,
            send_sem=sems.at[(0,) + index], recv_sem=sems.at[(1,) + index],
            device_id=device, device_id_type=MESH,
        )

    everyone = nlon * nchan * nlat
    me = (lon * nchan + chan) * nlat + lat
    barrier = pltpu.get_barrier_semaphore()

    @pl.loop(1, everyone)
    def _(d):
        peer = lax.rem(me + d, everyone)
        pl.semaphore_signal(
            barrier, inc=1, device_id_type=MESH,
            device_id=at(peer // (nchan * nlat), lax.rem(peer // nlat, nchan), lax.rem(peer, nlat)),
        )

    def edges(field, start):
        rows, lanes = 2 * H, field.shape[1]
        row = lax.broadcasted_iota(jnp.int32, (rows, lanes), 0)
        lane = lax.broadcasted_iota(jnp.int32, (rows, lanes), 1) + start * W
        want = jnp.where(row < H, row * W, (row - H) * W + W - 1)
        pick = jnp.where(lane == want, 1.0, 0.0).astype(BF)
        return nt(pick, field).astype(BF)

    def walk(start, count):
        return jnp.where(lat == 1, start, H - start - count)

    def cols(row, count):
        return pl.ds(pl.multiple_of(row * W, W), count * W)

    edge[...] = edges(x_ref[...], 0)
    mine = pl.ds(pl.multiple_of(chan * C, C), C)
    xs[1, mine, pl.ds(W, L)] = x_ref[...]
    rim = cols(lat * (H + 1), 1)
    for q in range(3):
        xs[q, :, rim] = jnp.zeros((CA, W), BF)
        gs[q, :, rim] = jnp.zeros((C, W), BF)
    pl.semaphore_wait(barrier, everyone - 1)

    from_row = cols(other * (H - 1), 1)
    to_row = rim
    halo_copies = []
    for d in range(nchan):
        there = lax.rem(chan + d, nchan)
        halo_copies.append(
            copy(x_ref.at[:, from_row], xs.at[1, mine, to_row], row_sem, (d,), at(lon, there, other))
        )
        for side in range(2):
            lon_to = lax.rem(lon + (nlon - 1 if side == 0 else 1), nlon)
            for dl in range(2):
                halo_copies.append(
                    copy(
                        edge.at[pl.ds(side * H, H)],
                        hx.at[chan, pl.ds(((1 - side) * 2 + dl) * H, H)],
                        col_sem, (d, side, dl),
                        at(lon_to, there, lat if dl == 0 else other),
                    )
                )
    for c in halo_copies:
        c.start()
    step = H // PIECES
    x_starts = [0] + [step * j + 1 for j in range(1, PIECES)] + [H]
    x_copies = []
    for j in range(PIECES):
        count = x_starts[j + 1] - x_starts[j]
        row = walk(x_starts[j], count)
        x_copies.append([
            copy(
                x_ref.at[:, cols(row, count)], xs.at[1, mine, cols(row + 1, count)],
                x_sem, (d, j), at(lon, lax.rem(chan + d, nchan), lat),
            )
            for d in range(1, nchan)
        ])
        for c in x_copies[j]:
            c.start()

    for t in range(9):
        w2[:, pl.ds(t * CA, CA)] = w_ref[pl.ds(t * C, C), :]
    wt[...] = jnp.transpose(w_ref[...])
    bias_col = jnp.transpose(jnp.broadcast_to(b_ref[...], (128, C)))[:, :1]

    def build_shifts(field, columns, start, count):
        lane = lax.broadcasted_iota(jnp.int32, columns.shape, 1)
        for i in range(count):
            r = start + i
            here = cols(r, 1)
            held = jnp.where(r == 0, 2 * H - 1, jnp.where(r == H + 1, H, r - 1))
            row = field[1, :, here]
            left = pltpu.roll(columns, lax.rem(W - held, W), 1)
            right = pltpu.roll(columns, lax.rem(2 * W - 1 - 2 * H - held, W), 1)
            field[0, :, here] = jnp.where(lane == 0, left, pltpu.roll(row, 1, 1))
            field[2, :, here] = jnp.where(lane == W - 1, right, pltpu.roll(row, W - 1, 1))

    def turned(blocks):
        have = sum(b.shape[0] for b in blocks)
        full = jnp.concatenate(blocks + [jnp.zeros((128 - have, C), BF)], axis=0)
        return jnp.transpose(full)

    for c in halo_copies:
        c.wait()
    for k in range(nchan):
        hc[pl.ds(k * C, C), :] = turned([hx[k]])

    ring = nlon * nlat
    spot = lon * nlat + lat
    group_rows = 3 * C
    half = R // 2
    quarter = half // nlon
    base = pl.multiple_of(lat * half, half)
    far = pl.ds(pl.multiple_of(other * half, half), half)
    core_copies, bias_copies, dx_copies = [], [], []
    dx_starts = [0] + [step * j - 1 for j in range(1, PIECES)] + [H]
    if R > group_rows:
        for g in range(3):
            dwp[g, pl.ds(group_rows, R - group_rows), :] = jnp.zeros((R - group_rows, CA), F32)
    grad_copies = []

    def input_grad(j):
        if j == 0:
            for c in grad_copies:
                c.wait()
            sides = turned([hg[0], hgo[0], hg[1], hgo[1]])
            build_shifts(gs, sides, other, H + 1)
        count = dx_starts[j + 1] - dx_starts[j]
        row = walk(dx_starts[j], count)
        stack = jnp.concatenate(
            [gs[2 - q, :, cols(row + 2 - p, count)] for p in range(3) for q in range(3)], axis=0
        )
        whole = jnp.dot(wt[...], stack, preferred_element_type=F32)
        dxf[:, cols(row, count)] = whole
        dxs[:, cols(row, count)] = whole.astype(BF)
        for d in range(1, nchan):
            there = lax.rem(chan + d, nchan)
            theirs = pl.ds(pl.multiple_of(there * C, C), C)
            c = copy(
                dxs.at[theirs, cols(row, count)], dxr.at[d, :, cols(row, count)],
                dx_sem, (d, j), at(lon, there, lat),
            )
            c.start()
            dx_copies.append(c)

    for j in range(PIECES):
        final = j == PIECES - 1
        for c in x_copies[j]:
            c.wait()
        count = x_starts[j + 1] - x_starts[j]
        if j == 0:
            build_shifts(xs, hc[...], jnp.where(lat == 1, 0, H + 1 - count), count + 1)
        else:
            build_shifts(xs, hc[...], walk(x_starts[j], count) + 1, count)
        row = walk(j * step, step)
        stack = jnp.concatenate(
            [xs[q, :, cols(row + p, step)] for p in range(3) for q in range(3)], axis=0
        )
        preact = jnp.dot(w2[...], stack, preferred_element_type=F32) + bias_col
        upstream = ct_ref[:, cols(row, step)].astype(F32)
        grad = (upstream * gelu_slope(preact)).astype(BF)
        gs[1, :, cols(row + 1, step)] = grad
        if final:
            gedge[...] = edges(gs[1, :, pl.ds(W, L)], 0)
            grad_copies.append(
                copy(gs.at[1, :, cols(other * (H - 1) + 1, 1)], gs.at[1, :, to_row], grow_sem, (0,), at(lon, chan, other))
            )
            for side in range(2):
                lon_to = lax.rem(lon + (nlon - 1 if side == 0 else 1), nlon)
                tile = gedge.at[pl.ds(side * H, H)]
                grad_copies.append(copy(tile, hg.at[1 - side], gcol_sem, (side,), at(lon_to, chan, lat)))
                grad_copies.append(copy(tile, hgo.at[1 - side], gother_sem, (side,), at(lon_to, chan, other)))
            for c in grad_copies:
                c.start()
        for p in range(3):
            for q in range(3):
                here = pl.ds(q * C, C)
                more = nt(grad, xs[q, :, cols(row + p, step)])
                dwp[p, here, :] = more if j == 0 else dwp[p, here, :] + more
            if final:
                dwsend[p] = dwp[p, far, :].astype(BF)
                c = copy(dwsend.at[p], dwcore.at[p], core_sem, (p,), at(lon, chan, other))
                c.start()
                core_copies.append(c)

    input_grad(0)
    rs_copies = []
    for g in range(3):
        core_copies[g].wait()
        summed = dwp[g, pl.ds(base, half), :] + dwcore[g].astype(F32)
        dwp[g, pl.ds(base, half), :] = summed
        zsend[g] = summed.astype(BF)
        rs_copies.append([])
        for d in range(1, nlon):
            there = lax.rem(lon + d, nlon)
            c = copy(
                zsend.at[g, pl.ds(pl.multiple_of(there * quarter, 16), quarter), :],
                zrecv.at[g, d], rs_sem, (g, d), at(there, chan, lat),
            )
            c.start()
            rs_copies[g].append(c)
    for j in range(1, PIECES):
        input_grad(j)
    bias[spot] = nt(jnp.ones((8, L), BF), gs[1, :, pl.ds(W, L)])
    for d in range(1, ring):
        peer = lax.rem(spot + d, ring)
        c = copy(bias.at[spot], bias.at[spot], bias_sem, (d,), at(peer // nlat, chan, lax.rem(peer, nlat)))
        c.start()
        bias_copies.append(c)
    own_rows = pl.ds(pl.multiple_of(base + lon * quarter, 16), quarter)
    ag_copies, fwd_copies = [], []
    for g in range(3):
        total = dwp[g, own_rows, :]
        for d in range(1, nlon):
            rs_copies[g][d - 1].wait()
            total = total + zrecv[g, d].astype(F32)
        gathered[g, own_rows, :] = total.astype(BF)
        ag_copies.append([])
        for d in range(1, nlon):
            c = copy(
                gathered.at[g, own_rows, :], gathered.at[g, own_rows, :], ag_sem, (g, d),
                at(lax.rem(lon + d, nlon), chan, lat),
            )
            c.start()
            ag_copies[g].append(c)

    def finish_dx(j):
        count = dx_starts[j + 1] - dx_starts[j]
        here = cols(walk(dx_starts[j], count), count)
        acc = dxf[mine, here]
        for d in range(1, nchan):
            dx_copies[j * (nchan - 1) + d - 1].wait()
            acc = acc + dxr[d, :, here].astype(F32)
        dx_ref[:, here] = acc.astype(BF)

    for j in range(PIECES - 1):
        finish_dx(j)
    for g in range(3):
        for d in range(nlon):
            if d > 0:
                ag_copies[g][d - 1].wait()
            source = lax.rem(lon + nlon - d, nlon)
            rows = pl.ds(pl.multiple_of(base + source * quarter, 16), quarter)
            c = copy(gathered.at[g, rows, :], gathered.at[g, rows, :], fwd_sem, (g, d), at(lon, chan, other))
            c.start()
            fwd_copies.append(c)
    finish_dx(PIECES - 1)
    for c in bias_copies:
        c.wait()
    db_ref[...] = jnp.sum(bias[...], axis=0)[:1]
    for c in fwd_copies:
        c.wait()
    dw_ref[...] = gathered[...]


def local(nlon, nchan, nlat, inputs, cotangent, weight, bias_vector):
    C, H, W = inputs.shape
    CA = weight.shape[3]
    L = H * W
    step = nlat * nlon * 16
    R = -(-3 * C // step) * step
    half = R // nlat
    sizes = (nlon, nchan, nlat, C, CA, H, W, R)
    wide = (H + 2) * W
    vmem = pl.BlockSpec(memory_space=pltpu.VMEM)
    dma = pltpu.SemaphoreType.DMA
    dx, dw, db = pl.pallas_call(
        functools.partial(kernel, sizes),
        out_shape=(
            jax.ShapeDtypeStruct((C, L), BF),
            jax.ShapeDtypeStruct((3, R, CA), BF),
            jax.ShapeDtypeStruct((1, C), F32),
        ),
        in_specs=[vmem] * 4,
        out_specs=(vmem,) * 3,
        scratch_shapes=[
            pltpu.VMEM((3, CA, wide), BF),
            pltpu.VMEM((nchan, 4 * H, C), BF),
            pltpu.VMEM((CA, 128), BF),
            pltpu.VMEM((2 * H, C), BF),
            pltpu.VMEM((C, 9 * CA), BF),
            pltpu.VMEM((CA, 9 * C), BF),
            pltpu.VMEM((3, C, wide), BF),
            pltpu.VMEM((2, H, C), BF),
            pltpu.VMEM((2, H, C), BF),
            pltpu.VMEM((2 * H, C), BF),
            pltpu.VMEM((3, R, CA), F32),
            pltpu.VMEM((3, half, CA), BF),
            pltpu.VMEM((3, half, CA), BF),
            pltpu.VMEM((3, half, CA), BF),
            pltpu.VMEM((3, nlon, half // nlon, CA), BF),
            pltpu.VMEM((3, R, CA), BF),
            pltpu.VMEM((nlon * nlat, 8, C), F32),
            pltpu.VMEM((CA, L), F32),
            pltpu.VMEM((CA, L), BF),
            pltpu.VMEM((nchan, C, L), BF),
            dma((2, nchan, PIECES)),
            dma((2, nchan)),
            dma((2, nchan, 2, 2)),
            dma((2, 1)),
            dma((2, 2)),
            dma((2, 2)),
            dma((2, 3)),
            dma((2, 3, nlon)),
            dma((2, 3, nlon)),
            dma((2, 3, nlon)),
            dma((2, nlon * nlat)),
            dma((2, nchan, PIECES)),
        ],
        compiler_params=pltpu.CompilerParams(
            collective_id=0, has_side_effects=True, vmem_limit_bytes=48 * 1024 * 1024
        ),
        cost_estimate=pl.CostEstimate(
            flops=3 * 2 * 9 * C * CA * L, bytes_accessed=4 * C * L * 2, transcendentals=2 * C * L
        ),
        name="conv_backward",
    )(
        inputs.reshape(C, L),
        cotangent.reshape(C, L),
        weight.reshape(9 * C, CA),
        bias_vector.reshape(1, C),
    )
    weight_grad = dw[:, : 3 * C].astype(F32).reshape(3, 3, C, CA)
    return dx.reshape(C, H, W), weight_grad, db.reshape(C)


def solution(mesh):
    shape = mesh.shape
    placed = (
        P("chan", ("groups", "lat"), "lon"),
        P("chan", ("groups", "lat"), "lon"),
        P(None, None, "chan", None),
        P("chan"),
    )
    return jax.shard_map(
        functools.partial(local, shape["lon"], shape["chan"], shape["lat"]),
        mesh=mesh,
        in_specs=placed,
        out_specs=(
            P("chan", ("groups", "lat"), "lon"),
            P("groups", None, "chan", None),
            P(("groups", "chan")),
        ),
        check_vma=False,
    )
```
